768 devices in a mesh: dp: 8 (over y_hi, core), basis: 96 (over x, y_lo, z).
Axes of the slice: x: 4, y: 8 (y_hi: 4, y_lo: 2; y = y_hi * 2 + y_lo), z: 12, core: 2. Of those that a mesh axis runs over, the one named last changes fastest.
Arguments:
- out_grads: bfloat16 [15360, 2048], P(('dp', 'basis')), may hold values from -6 to 6
- inputs: bfloat16 [2048, 6144], P('dp'), may hold values from -6 to 6
- basis_grads: bfloat16 [15360, 15360], P('dp', 'basis'), may hold values from -0.046875 to 0.046875
- basis_inputs: bfloat16 [6144, 6144], P(None, 'basis'), may hold values from -0.078125 to 0.078125
- counts: int32 [16], P('dp'), may hold values from 1 to 128, 1536 in all
Outputs:
- corrections: float32 [15360, 6144], P('basis', 'dp')
The draws below stay inside these ranges and needn't reach their ends.
Inputs may be any that keep to these rules, and one draw needn't show every extreme that they name: `counts`: some example has all 128 slots live.
All inputs are finite; a program needn't handle non-finite values. No bound on the sum of `counts` on one device may be relied on, other than what follows from the above.
Results may differ from the reference program's by a relative error of at most 0.0023.
Values may be sent and summed in bfloat16 or wider, within the bound.
A program may use at most 64 MiB of HBM per device.

```python
import math
import jax
import jax.numpy as jnp
import numpy as np
from jax import lax

HG = 15360
HA = 6144
SEQ = 128
EXAMPLES = 16
TOKENS = 2048


def steps_of(stream_key, extent, pieces, least, top_value):
    def one(dim, parts):
        heights = jax.random.uniform(jax.random.fold_in(jax.random.fold_in(stream_key, 6), dim), (parts,), jnp.float32, least / len(pieces), top_value / len(pieces))
        return jnp.repeat(jnp.exp(heights), extent[dim] // parts).reshape((-1,) + (1,) * (len(extent) - dim - 1))

    factor_of = one(*pieces[0])
    for cut in pieces[1:]:
        factor_of = factor_of * one(*cut)
    return factor_of


def profile(count, total, most, lean):
    loads = [(1 << 20) // math.isqrt(rank ** lean) + 1 for rank in range(2, count + 1)]
    spare, holding = total - most - (count - 1), [1] * (count - 1)
    while spare > 0:
        movable = [i for i in range(count - 1) if holding[i] < most]
        pool, remaining = sum([loads[i] for i in movable]), spare
        for i in movable:
            addition = min(most - holding[i], max(1, remaining * loads[i] // pool), spare)
            holding[i] = holding[i] + addition
            spare = spare - addition
    return np.array([most] + holding)


def ragged_sizes(rng, number_of, total, most, slope):
    if number_of == 2:
        one = jax.random.randint(rng, (), max(1, total - most), min(most, total - 1) + 1)
        return jnp.stack([one, total - one])
    sizes = jnp.asarray(profile(number_of, total, most, slope), jnp.int32)
    pairs = (number_of - 1) // 2
    donor, sink = sizes[1:1 + 2 * pairs:2], sizes[2:2 + 2 * pairs:2]
    room = jnp.minimum(donor - 1, most - sink)
    moved = jax.random.randint(jax.random.fold_in(rng, 1), (pairs,), 0, 1 << 20) % (room + 1)
    sizes = sizes.at[1:1 + 2 * pairs:2].set(donor - moved).at[2:2 + 2 * pairs:2].set(sink + moved)
    return sizes[jax.random.permutation(jax.random.fold_in(rng, 2), number_of)]


def gaussian(own_key, dims, width, most, pieces=(), kind=jnp.bfloat16):
    values = jax.random.normal(own_key, dims, jnp.float32) * width
    if len(pieces) > 0:
        values = steps_of(own_key, dims, pieces, -0.22, 0.18) * values
    return jnp.clip(values, min=-most, max=most).astype(kind)


def setup_inputs(seed: int = 0) -> dict:
    key_of = jax.random.split(jax.random.key(seed), 6)
    return {
        "out_grads": gaussian(key_of[0], (HG, TOKENS), 1.0, 6.0, ((0, 768),)),
        "inputs": gaussian(key_of[1], (TOKENS, HA), 1.0, 6.0, ((0, 8),)),
        "basis_grads": gaussian(key_of[2], (HG, HG), HG ** -0.5, 0.046875, ((0, 8), (1, 96))),
        "basis_inputs": gaussian(key_of[3], (HA, HA), HA ** -0.5, 0.078125, ((1, 96),)),
        "counts": ragged_sizes(key_of[4], EXAMPLES, EXAMPLES * 96, SEQ, 2).astype(jnp.int32),
    }


def reference(out_grads, inputs, basis_grads, basis_inputs, counts):
    rotated_grads = jnp.dot(out_grads.T, basis_grads, preferred_element_type=jnp.float32).astype(jnp.bfloat16)
    slots = jnp.arange(SEQ, dtype=jnp.int32)
    keep = slots[None, :] < counts.astype(jnp.int32)[:, None]
    shaped = inputs.reshape(EXAMPLES, SEQ, HA)
    masked = jnp.where(keep[:, :, None], shaped, jnp.zeros((), inputs.dtype)).reshape(TOKENS, HA)
    rotated_inputs = jnp.dot(masked, basis_inputs, preferred_element_type=jnp.float32).astype(jnp.bfloat16)

    def step(total, pair):
        grads_block, inputs_block = pair
        product = jnp.dot(grads_block.T, inputs_block, preferred_element_type=jnp.float32)
        return total + product * product, None

    start = jnp.zeros((HG, HA), jnp.float32)
    total, unused = lax.scan(step, start, (rotated_grads.reshape(EXAMPLES, SEQ, HG), rotated_inputs.reshape(EXAMPLES, SEQ, HA)))
    return total * (1.0 / (EXAMPLES * SEQ))
```

```python
import jax
import jax.numpy as jnp
from jax import lax
from jax.experimental import pallas as pl
from jax.experimental.pallas import tpu as pltpu
from jax.sharding import PartitionSpec as P

MESH = pl.DeviceIdType.MESH
BF16, F32 = jnp.bfloat16, jnp.float32

NX, NL, NZ, NH, NC = 4, 2, 12, 4, 2
SLOTS = NL * NZ
UNITS = 20
GROUP = NX * UNITS
BLOCK = SLOTS * GROUP
COLS = 160
HALF = COLS // 2
QUARTER = 512
CHUNKS = 2
TW = QUARTER // CHUNKS
SLOT = 128
FEATS = 64
WIDE = NZ * FEATS
TOK = 256
DEPTH = 6144
FACTOR = 1.0 / 2048.0
NSEM = 128


def dot(a, b, dims=((1,), (0,))):
    return lax.dot_general(a, b, (dims, ((), ())), preferred_element_type=F32)


def kernel(
    g_ref, b_ref, in_ref, bi_ref, cnt_ref, out_ref,
    gs, ga, gb, bb, iv, biv, rt, rb, cb, cr, ss, sr, ab, acc, o1s, o1r, o2s, o2r,
    ssem, rsem, lsem,
):
    d, b = lax.axis_index("dp"), lax.axis_index("basis")
    yh, c = d // NC, d % NC
    x, yl, z = b // SLOTS, (b // NZ) % NL, b % NZ
    slot = yl * NZ + z

    def dev(yh=yh, c=c, x=x, yl=yl, z=z):
        return (yh * NC + c, x * SLOTS + yl * NZ + z)

    zr, zl = lax.rem(z + 1, NZ), lax.rem(z + NZ - 1, NZ)
    xr, xl, xo = lax.rem(x + 1, NX), lax.rem(x + 3, NX), lax.rem(x + 2, NX)
    yhs = [lax.rem(yh + r, NH) for r in range(NH)]
    pair_y, pair_c = dev(yl=1 - yl), dev(c=1 - c)
    right, left = dev(z=zr), dev(z=zl)
    swap = dev(yh=x, c=yl, x=yh, yl=c)
    lone = jnp.logical_and(yh == x, c == yl)

    barrier = pltpu.get_barrier_semaphore()
    peers = [right, left, pair_y, pair_c]
    peers += [dev(x=xr), dev(x=xl), dev(x=xo)] + [dev(yh=yhs[r]) for r in (1, 2, 3)]
    for peer in peers:
        pl.semaphore_signal(barrier, inc=1, device_id=peer, device_id_type=MESH)

    @pl.when(jnp.logical_not(lone))
    def _():
        pl.semaphore_signal(barrier, inc=1, device_id=swap, device_id_type=MESH)

    keys = {}
    sent = []

    def copy(key, src, dst, target):
        i = keys.setdefault(key, len(keys))
        return pltpu.make_async_remote_copy(
            src_ref=src, dst_ref=dst, send_sem=ssem.at[i], recv_sem=rsem.at[i],
            device_id=target, device_id_type=MESH,
        )

    def send(key, src, dst, target):
        cp = copy(key, src, dst, target)
        cp.start()
        sent.append(cp)

    def got(key, ref):
        copy(key, ref, ref, pair_c).wait_recv()

    load_in = pltpu.make_async_copy(in_ref, iv, lsem.at[0])
    load_bi = pltpu.make_async_copy(bi_ref, biv, lsem.at[1])
    load_in.start()
    load_bi.start()

    gs[...] = jnp.zeros_like(gs)
    for q in range(NX):
        gs[q, 0:UNITS, :] = g_ref[:, q * QUARTER : (q + 1) * QUARTER]

    pl.semaphore_wait(barrier, jnp.where(lone, len(peers), len(peers) + 1))

    for n, xt in enumerate((xr, xl, xo)):
        send(("a", n), gs.at[xt], ga.at[x], dev(x=xt))
    ga[x] = gs[x]

    row = lax.broadcasted_iota(jnp.int32, (COLS, 8 * GROUP), 0)
    lane = lax.broadcasted_iota(jnp.int32, (COLS, 8 * GROUP), 1)
    place = row + 60 * ((row * 3277) >> 16)
    for part in range(3):
        total = None
        for q in range(NX):
            pick = jnp.where(lane == place + 20 * q, 1.0, 0.0).astype(BF16)
            start = q * (BLOCK // NX) + part * COLS
            term = dot(b_ref[start : start + COLS, :], pick, ((0,), (0,)))
            total = term if total is None else total + term
        bb[x, :, part * 640 : (part + 1) * 640] = total.astype(BF16)
    for h in range(2):
        rows = pl.ds(h * HALF, HALF)
        send(("b", "r", h), bb.at[x, rows], bb.at[x, rows], dev(x=xr))
        send(("b", "l", h), bb.at[x, rows], bb.at[x, rows], dev(x=xl))

    class Item:
        def __init__(self, name, ref, both, far):
            self.name, self.ref, self.both, self.far = name, ref, both, far

        def at(self, mine, shift):
            col = yl if mine else 1 - yl
            return self.ref(col * NZ + lax.rem(z + shift + 2 * NZ, NZ))

        def hop(self, way, mine, k, shift):
            ref = self.at(mine, shift)
            send((self.name, way, mine, k), ref, ref, right if way == "r" else left)

        def across(self, shift):
            ref = self.at(True, shift)
            send((self.name, "y", shift), ref, ref, pair_y)

        def last(self, way, mine):
            return 6 if (way == self.far) == mine else 5

        def begin(self):
            self.hop("r", True, 1, 0)
            self.hop("l", True, 1, 0)
            self.across(0)

        def begin_other(self):
            if self.both:
                got((self.name, "y", 0), self.at(False, 0))
                self.hop("r", False, 1, 0)
                self.hop("l", False, 1, 0)

        def step(self, k):
            for mine in (True, False) if self.both else (True,):
                for way, sign in (("r", -1), ("l", 1)):
                    if k <= self.last(way, mine):
                        got((self.name, way, mine, k), self.at(mine, sign * k))
                        if k < self.last(way, mine):
                            self.hop(way, mine, k + 1, sign * k)
                        if not self.both:
                            self.across(sign * k)

        def end(self):
            if not self.both:
                shifts = [0]
                for k in range(1, 7):
                    shifts += [s * k for w, s in (("r", -1), ("l", 1)) if k <= self.last(w, True)]
                for shift in shifts:
                    got((self.name, "y", shift), self.at(False, shift))

    grads = [
        Item("g0", lambda s: gb.at[0, s], False, "r"),
        Item("g1", lambda s: gb.at[1, s], True, "r"),
    ]
    rot = Item("r", lambda s: rb.at[s], False, "l")

    for n, xt in enumerate((xl, xr, xo)):
        got(("a", n), ga.at[xt])
    prow = lax.broadcasted_iota(jnp.int32, (GROUP, NX * 32), 0)
    plane = lax.broadcasted_iota(jnp.int32, (GROUP, NX * 32), 1)
    unit = plane & 31
    hit = jnp.logical_and(prow == (plane >> 5) * UNITS + unit, unit < UNITS)
    pick = jnp.where(hit, 1.0, 0.0).astype(BF16)
    packed = dot(pick, ga[...].reshape(NX * 32, QUARTER)).astype(BF16)
    for ch in range(CHUNKS):
        gb[ch, slot] = packed[:, ch * TW : (ch + 1) * TW]
        grads[ch].begin()

    load_bi.wait()
    load_in.wait()

    def slab(i, total):
        at = pl.ds(pl.multiple_of(i * 1536, 1536), 1536)
        return total + dot(iv[:, at], biv[at, :])

    tile = lax.fori_loop(0, DEPTH // 1536, slab, jnp.zeros((TOK, FEATS), F32))
    token = lax.broadcasted_iota(jnp.int32, (TOK, FEATS), 0)
    live = jnp.where(token < SLOT, cnt_ref[0], cnt_ref[1])
    tile = jnp.where((token & (SLOT - 1)) < live, tile, 0.0)
    rt[...] = tile.T.astype(BF16)
    own_copy = pltpu.make_async_copy(rt, rb.at[slot], lsem.at[2])

    swap_copy = copy(("swap",), rt, rb.at[c * NZ + z], swap)

    @pl.when(lone)
    def _():
        own_copy.start()
        own_copy.wait()

    @pl.when(jnp.logical_not(lone))
    def _():
        swap_copy.start()

    grads[1].begin_other()

    def rot_begin():
        @pl.when(jnp.logical_not(lone))
        def _():
            got(("swap",), rb.at[slot])

        rot.begin()

    for it in range(1, 9):
        for item in grads:
            if it <= 6:
                item.step(it)
        if it == 1:
            rot_begin()
        if 2 <= it <= 7:
            rot.step(it - 1)
        if it == 4:
            top = pl.ds(0, HALF)
            got(("b", "r", 0), bb.at[xl, top])
            send(("b", "rr"), bb.at[xl, top], bb.at[xl, top], dev(x=xr))
            got(("b", "l", 0), bb.at[xr, top])
            low = pl.ds(HALF, HALF)
            got(("b", "l", 1), bb.at[xr, low])
            send(("b", "ll"), bb.at[xr, low], bb.at[xr, low], dev(x=xl))
            got(("b", "r", 1), bb.at[xl, low])
    grads[0].end()
    got(("b", "rr"), bb.at[xo, pl.ds(0, HALF)])
    got(("b", "ll"), bb.at[xo, pl.ds(HALF, HALF)])

    def multiply(ch):
        weights = gb[ch].reshape(BLOCK, TW)
        for q in range(NX):
            part = dot(bb[q], weights)
            cb[ch, 0, q] = part[:HALF]
            cb[ch, 1, q] = part[HALF:]
        send(("c", ch), cb.at[ch, 1 - c], cr.at[ch], pair_c)

    def scatter(ch):
        got(("c", ch), cr.at[ch])
        for q in range(NX):
            ss[ch, q] = (cb[ch, c, q] + cr[ch, q]).astype(BF16)
        for r in (1, 2, 3):
            send(("s", ch, r), ss.at[ch, yhs[r]], sr.at[ch, r - 1], dev(yh=yhs[r]))

    def spread(ch):
        total = cb[ch, c, yh] + cr[ch, yh]
        for r in (1, 2, 3):
            got(("s", ch, r), sr.at[ch, r - 1])
            total = total + sr[ch, r - 1].astype(F32)
        ab[ch, yh, c] = total.astype(BF16)
        mine = ab.at[ch, yh, c]
        for r in (1, 2, 3):
            send(("t", ch, r), mine, mine, dev(yh=yhs[r]))
        send(("u", ch, 0), mine, mine, pair_c)

    def collect(ch):
        for r in (1, 3, 2):
            ref = ab.at[ch, yhs[NH - r], c]
            got(("t", ch, r), ref)
            send(("u", ch, r), ref, ref, pair_c)
        for r in range(NH):
            got(("u", ch, r), ab.at[ch, yhs[(NH - r) % NH], 1 - c])

    def products(ch, xt):
        for h in range(2):
            for f in range(3):
                total = None
                for e in range(TW // SLOT):
                    at = slice(e * SLOT, (e + 1) * SLOT)
                    first = ch * NZ + f * 4
                    rows = rb[first : first + 4, :, at].reshape(4 * FEATS, SLOT)
                    term = dot(ab[ch, xt, h, :, at], rows, ((1,), (1,)))
                    total = term * term if total is None else total + term * term
                where = (xt, pl.ds(h * HALF, HALF), pl.ds(f * 256, 256))
                acc[where] = total if ch == 0 else acc[where] + total

    for ch in range(CHUNKS):
        multiply(ch)
    for ch in range(CHUNKS):
        scatter(ch)
    for ch in range(CHUNKS):
        spread(ch)
    rot.end()
    collect(0)
    for xt in (xo, xr, xl, x):
        products(0, xt)
    collect(1)

    top, low = pl.ds(0, HALF), pl.ds(HALF, HALF)
    products(1, xo)
    o1s[0] = acc[xo, top].astype(BF16)
    send(("o1", "r"), o1s.at[0], o1r.at[0], dev(x=xr))
    o1s[1] = acc[xo, low].astype(BF16)
    send(("o1", "l"), o1s.at[1], o1r.at[1], dev(x=xl))
    products(1, xr)
    o2s[0, 1] = acc[xr, low].astype(BF16)
    send(("o2", "r", 1), o2s.at[0, 1], o2r.at[0, 1], dev(x=xr))
    products(1, xl)
    o2s[1, 0] = acc[xl, top].astype(BF16)
    send(("o2", "l", 0), o2s.at[1, 0], o2r.at[1, 0], dev(x=xl))
    got(("o1", "r"), o1r.at[0])
    o2s[0, 0] = (acc[xr, top] + o1r[0].astype(F32)).astype(BF16)
    send(("o2", "r", 0), o2s.at[0, 0], o2r.at[0, 0], dev(x=xr))
    got(("o1", "l"), o1r.at[1])
    o2s[1, 1] = (acc[xl, low] + o1r[1].astype(F32)).astype(BF16)
    send(("o2", "l", 1), o2s.at[1, 1], o2r.at[1, 1], dev(x=xl))
    products(1, x)
    for w, way in ((0, "r"), (1, "l")):
        for h in (1 - w, w):
            got(("o2", way, h), o2r.at[w, h])
    for h in range(2):
        rows = pl.ds(h * HALF, HALF)
        total = acc[x, rows] + o2r[0, h].astype(F32) + o2r[1, h].astype(F32)
        out_ref[rows, :] = total * FACTOR

    for cp in sent:
        cp.wait_send()

    @pl.when(jnp.logical_not(lone))
    def _():
        swap_copy.wait_send()

    assert len(keys) <= NSEM


def shards(out_grads, inputs, basis_grads, basis_inputs, counts):
    vmem = pl.BlockSpec(memory_space=pltpu.VMEM)
    hbm = pl.BlockSpec(memory_space=pl.ANY)
    return pl.pallas_call(
        kernel,
        out_shape=jax.ShapeDtypeStruct((COLS, WIDE), F32),
        in_specs=[vmem, vmem, hbm, hbm, pl.BlockSpec(memory_space=pltpu.SMEM)],
        out_specs=vmem,
        scratch_shapes=[
            pltpu.VMEM((NX, 32, QUARTER), BF16),
            pltpu.VMEM((NX, 32, QUARTER), BF16),
            pltpu.VMEM((CHUNKS, SLOTS, GROUP, TW), BF16),
            pltpu.VMEM((NX, COLS, BLOCK), BF16),
            pltpu.VMEM((TOK, DEPTH), BF16),
            pltpu.VMEM((DEPTH, FEATS), BF16),
            pltpu.VMEM((FEATS, TOK), BF16),
            pltpu.VMEM((SLOTS, FEATS, TOK), BF16),
            pltpu.VMEM((CHUNKS, 2, NX, HALF, TW), F32),
            pltpu.VMEM((CHUNKS, NX, HALF, TW), F32),
            pltpu.VMEM((CHUNKS, NX, HALF, TW), BF16),
            pltpu.VMEM((CHUNKS, 3, HALF, TW), BF16),
            pltpu.VMEM((CHUNKS, NH, NC, HALF, TW), BF16),
            pltpu.VMEM((NX, COLS, WIDE), F32),
            pltpu.VMEM((2, HALF, WIDE), BF16),
            pltpu.VMEM((2, HALF, WIDE), BF16),
            pltpu.VMEM((2, 2, HALF, WIDE), BF16),
            pltpu.VMEM((2, 2, HALF, WIDE), BF16),
            pltpu.SemaphoreType.DMA((NSEM,)),
            pltpu.SemaphoreType.DMA((NSEM,)),
            pltpu.SemaphoreType.DMA((4,)),
        ],
        compiler_params=pltpu.CompilerParams(
            collective_id=0, has_side_effects=True, vmem_limit_bytes=40 * 1024 * 1024
        ),
        cost_estimate=pl.CostEstimate(
            flops=2_200_000_000, bytes_accessed=10_000_000, transcendentals=0
        ),
    )(out_grads, basis_grads, inputs, basis_inputs, counts)


def solution(mesh):
    placed = (P(("dp", "basis"), None), P("dp", None), P("dp", "basis"), P(None, "basis"), P("dp"))
    return jax.shard_map(
        shards, mesh=mesh, in_specs=placed, out_specs=P("basis", "dp"), check_vma=False
    )
```

```python
import jax
import jax.numpy as jnp
from jax import lax
from jax.experimental import pallas as pl
from jax.experimental.pallas import tpu as pltpu
from jax.sharding import PartitionSpec as P

MESH = pl.DeviceIdType.MESH
BF16, F32 = jnp.bfloat16, jnp.float32

NX, NL, NZ, NH, NC = 4, 2, 12, 4, 2
SLOTS = NL * NZ
UNITS = 20
GROUP = NX * UNITS
BLOCK = SLOTS * GROUP
COLS = 160
HALF = COLS // 2
QUARTER = 512
CHUNKS = 2
TW = QUARTER // CHUNKS
SLOT = 128
FEATS = 64
WIDE = NZ * FEATS
TOK = 256
DEPTH = 6144
FACTOR = 1.0 / 2048.0
NSEM = 160


def dot(a, b, dims=((1,), (0,))):
    return lax.dot_general(a, b, (dims, ((), ())), preferred_element_type=F32)


def kernel(
    g_ref, b_ref, in_ref, bi_ref, cnt_ref, out_ref,
    gv, gs, ga, gb, bb, bv, picks, iv, biv, rt, rb, cb, cr, ss, sr, ab, acc, o1s, o1r, o2s, o2r,
    ssem, rsem, lsem,
):
    d, b = lax.axis_index("dp"), lax.axis_index("basis")
    yh, c = d // NC, d % NC
    x, yl, z = b // SLOTS, (b // NZ) % NL, b % NZ
    slot = yl * NZ + z

    def dev(yh=yh, c=c, x=x, yl=yl, z=z):
        return (yh * NC + c, x * SLOTS + yl * NZ + z)

    zr, zl = lax.rem(z + 1, NZ), lax.rem(z + NZ - 1, NZ)
    xr, xl, xo = lax.rem(x + 1, NX), lax.rem(x + 3, NX), lax.rem(x + 2, NX)
    yhs = [lax.rem(yh + r, NH) for r in range(NH)]
    pair_y, pair_c = dev(yl=1 - yl), dev(c=1 - c)
    right, left = dev(z=zr), dev(z=zl)
    swap = dev(yh=x, c=yl, x=yh, yl=c)
    lone = jnp.logical_and(yh == x, c == yl)

    barrier = pltpu.get_barrier_semaphore()
    peers = [right, left, pair_y, pair_c]
    peers += [dev(x=n, yl=m) for n in (xr, xl, xo) for m in (yl, 1 - yl)]
    peers += [dev(yh=yhs[r]) for r in (1, 2, 3)]
    for peer in peers:
        pl.semaphore_signal(barrier, inc=1, device_id=peer, device_id_type=MESH)

    @pl.when(jnp.logical_not(lone))
    def _():
        pl.semaphore_signal(barrier, inc=1, device_id=swap, device_id_type=MESH)

    keys = {}
    sent = []

    def copy(key, src, dst, target):
        i = keys.setdefault(key, len(keys))
        return pltpu.make_async_remote_copy(
            src_ref=src, dst_ref=dst, send_sem=ssem.at[i], recv_sem=rsem.at[i],
            device_id=target, device_id_type=MESH,
        )

    def send(key, src, dst, target):
        cp = copy(key, src, dst, target)
        cp.start()
        sent.append(cp)

    def got(key, ref):
        copy(key, ref, ref, pair_c).wait_recv()

    load_in = pltpu.make_async_copy(in_ref, iv, lsem.at[0])
    load_bi = pltpu.make_async_copy(bi_ref, biv, lsem.at[1])
    load_g = pltpu.make_async_copy(g_ref, gv, lsem.at[2])
    load_b = pltpu.make_async_copy(b_ref, bv, lsem.at[3])
    for load in (load_g, load_b, load_bi, load_in):
        load.start()

    gs[...] = jnp.zeros_like(gs)
    load_g.wait()
    for q in range(NX):
        gs[q, 0:UNITS, :] = gv[:, q * QUARTER : (q + 1) * QUARTER]

    pl.semaphore_wait(barrier, jnp.where(lone, len(peers), len(peers) + 1))

    for n, xt in enumerate((xr, xl, xo)):
        send(("a", n, 0), gs.at[xt], ga.at[0, x], dev(x=xt))
        send(("a", n, 1), gs.at[xt], ga.at[1, x], dev(x=xt, yl=1 - yl))
    send(("a", 3, 1), gs.at[x], ga.at[1, x], pair_y)
    ga[0, x] = gs[x]

    load_b.wait()
    row = lax.broadcasted_iota(jnp.int32, (COLS, 8 * GROUP), 0)
    lane = lax.broadcasted_iota(jnp.int32, (COLS, 8 * GROUP), 1)
    place = row + 60 * ((row * 3277) >> 16)
    for q in range(NX):
        picks[q] = jnp.where(lane == place + UNITS * q, 1.0, 0.0).astype(BF16)
    for part in range(3):
        total = None
        for q in range(NX):
            start = q * (BLOCK // NX) + part * COLS
            term = dot(bv[:, start : start + COLS], picks[q])
            total = term if total is None else total + term
        bb[x, :, part * 640 : (part + 1) * 640] = total.astype(BF16)
    for h in range(2):
        for way, half, xt in (("r", h, xr), ("l", 1 - h, xl)):
            ref = bb.at[x, pl.ds(half * HALF, HALF)]
            send(("b", way, half), ref, ref, dev(x=xt))

    class Item:
        def __init__(self, name, ref, both, far):
            self.name, self.ref, self.both, self.far = name, ref, both, far

        def at(self, mine, shift):
            col = yl if mine else 1 - yl
            return self.ref(col * NZ + lax.rem(z + shift + 2 * NZ, NZ))

        def hop(self, way, mine, k, shift):
            ref = self.at(mine, shift)
            send((self.name, way, mine, k), ref, ref, right if way == "r" else left)

        def across(self, shift):
            ref = self.at(True, shift)
            send((self.name, "y", shift), ref, ref, pair_y)

        def last(self, way, mine):
            return 6 if (way == self.far) == mine else 5

        def begin(self, mine):
            if mine or self.both:
                self.hop("r", mine, 1, 0)
                self.hop("l", mine, 1, 0)

        def step(self, k):
            for mine in (True, False) if self.both else (True,):
                for way, sign in (("r", -1), ("l", 1)):
                    if k <= self.last(way, mine):
                        got((self.name, way, mine, k), self.at(mine, sign * k))
                        if k < self.last(way, mine):
                            self.hop(way, mine, k + 1, sign * k)
                        if not self.both:
                            self.across(sign * k)

        def end(self):
            if not self.both:
                shifts = []
                for k in range(1, 7):
                    shifts += [s * k for w, s in (("r", -1), ("l", 1)) if k <= self.last(w, True)]
                for shift in shifts:
                    got((self.name, "y", shift), self.at(False, shift))

    grads = [
        Item("g0", lambda s: gb.at[0, s], False, "r"),
        Item("g1", lambda s: gb.at[1, s], True, "r"),
    ]
    rot = Item("r", lambda s: rb.at[s], True, "l")

    load_bi.wait()
    load_in.wait()

    def slab(i, total):
        at = pl.ds(pl.multiple_of(i * 1536, 1536), 1536)
        return total + dot(iv[:, at], biv[:, at], ((1,), (1,)))

    tile = lax.fori_loop(0, DEPTH // 1536, slab, jnp.zeros((TOK, FEATS), F32))
    token = lax.broadcasted_iota(jnp.int32, (TOK, FEATS), 0)
    live = jnp.where(token < SLOT, cnt_ref[0], cnt_ref[1])
    tile = jnp.where((token & (SLOT - 1)) < live, tile, 0.0)
    rt[...] = tile.T.astype(BF16)
    own_copy = pltpu.make_async_copy(rt, rb.at[slot], lsem.at[4])

    swap_copy = copy(("swap",), rt, rb.at[c * NZ + z], swap)

    @pl.when(lone)
    def _():
        own_copy.start()
        own_copy.wait()

    @pl.when(jnp.logical_not(lone))
    def _():
        swap_copy.start()

    for n, xt in enumerate((xl, xr, xo)):
        got(("a", n, 0), ga.at[0, xt])
        got(("a", n, 1), ga.at[1, xt])
    got(("a", 3, 1), ga.at[1, x])
    prow = lax.broadcasted_iota(jnp.int32, (GROUP, NX * 32), 0)
    plane = lax.broadcasted_iota(jnp.int32, (GROUP, NX * 32), 1)
    unit = plane & 31
    hit = jnp.logical_and(prow == (plane >> 5) * UNITS + unit, unit < UNITS)
    pick = jnp.where(hit, 1.0, 0.0).astype(BF16)
    for side, where in ((0, slot), (1, (1 - yl) * NZ + z)):
        packed = dot(pick, ga[side].reshape(NX * 32, QUARTER)).astype(BF16)
        for ch in range(CHUNKS):
            gb[ch, where] = packed[:, ch * TW : (ch + 1) * TW]
            grads[ch].begin(side == 0)


    def rot_begin():
        @pl.when(jnp.logical_not(lone))
        def _():
            got(("swap",), rb.at[slot])

        rot.begin(True)
        rot.across(0)

    def rot_other():
        got(("r", "y", 0), rot.at(False, 0))
        rot.begin(False)

    top, low = pl.ds(0, HALF), pl.ds(HALF, HALF)
    for it in range(1, 7):
        for item in grads:
            item.step(it)
        if it == 2:
            rot_begin()
        if it == 3:
            rot_other()
        if it >= 4:
            rot.step(it - 3)
        if it == 3:
            got(("b", "r", 0), bb.at[xl, top])
            send(("b", "rr"), bb.at[xl, top], bb.at[xl, top], dev(x=xr))
            got(("b", "l", 1), bb.at[xr, low])
            send(("b", "ll"), bb.at[xr, low], bb.at[xr, low], dev(x=xl))
        if it == 5:
            got(("b", "l", 0), bb.at[xr, top])
            got(("b", "r", 1), bb.at[xl, low])
    grads[0].end()
    got(("b", "rr"), bb.at[xo, pl.ds(0, HALF)])
    got(("b", "ll"), bb.at[xo, pl.ds(HALF, HALF)])

    def multiply(ch):
        weights = gb[ch].reshape(BLOCK, TW)
        for q in range(NX):
            part = dot(bb[q], weights)
            cb[ch, 0, q] = part[:HALF]
            cb[ch, 1, q] = part[HALF:]
        send(("c", ch), cb.at[ch, 1 - c], cr.at[ch], pair_c)

    def scatter(ch):
        got(("c", ch), cr.at[ch])
        for q in range(NX):
            ss[ch, q] = (cb[ch, c, q] + cr[ch, q]).astype(BF16)
        for r in (1, 2, 3):
            send(("s", ch, r), ss.at[ch, yhs[r]], sr.at[ch, r - 1], dev(yh=yhs[r]))

    def spread(ch):
        total = cb[ch, c, yh] + cr[ch, yh]
        for r in (1, 2, 3):
            got(("s", ch, r), sr.at[ch, r - 1])
            total = total + sr[ch, r - 1].astype(F32)
        ab[ch, yh, c] = total.astype(BF16)
        mine = ab.at[ch, yh, c]
        for r in (1, 2, 3):
            send(("t", ch, r), mine, mine, dev(yh=yhs[r]))
        send(("u", ch, 0), mine, mine, pair_c)

    def collect(ch):
        for r in (1, 3, 2):
            ref = ab.at[ch, yhs[NH - r], c]
            got(("t", ch, r), ref)
            send(("u", ch, r), ref, ref, pair_c)
        for r in range(NH):
            got(("u", ch, r), ab.at[ch, yhs[(NH - r) % NH], 1 - c])

    def products(ch, xt):
        for h in range(2):
            for f in range(3):
                total = None
                for e in range(TW // SLOT):
                    at = slice(e * SLOT, (e + 1) * SLOT)
                    first = ch * NZ + f * 4
                    rows = rb[first : first + 4, :, at].reshape(4 * FEATS, SLOT)
                    term = dot(ab[ch, xt, h, :, at], rows, ((1,), (1,)))
                    total = term * term if total is None else total + term * term
                where = (xt, pl.ds(h * HALF, HALF), pl.ds(f * 256, 256))
                acc[where] = total if ch == 0 else acc[where] + total

    for ch in range(CHUNKS):
        multiply(ch)
    rot.step(4)
    for ch in range(CHUNKS):
        scatter(ch)
    rot.step(5)
    for ch in range(CHUNKS):
        spread(ch)
    rot.step(6)
    collect(0)
    for xt in (xo, xr, xl, x):
        products(0, xt)
    collect(1)

    products(1, xo)
    o1s[0] = acc[xo, top].astype(BF16)
    send(("o1", "r"), o1s.at[0], o1r.at[0], dev(x=xr))
    o1s[1] = acc[xo, low].astype(BF16)
    send(("o1", "l"), o1s.at[1], o1r.at[1], dev(x=xl))
    products(1, xr)
    o2s[0, 1] = acc[xr, low].astype(BF16)
    send(("o2", "r", 1), o2s.at[0, 1], o2r.at[0, 1], dev(x=xr))
    products(1, xl)
    o2s[1, 0] = acc[xl, top].astype(BF16)
    send(("o2", "l", 0), o2s.at[1, 0], o2r.at[1, 0], dev(x=xl))
    got(("o1", "r"), o1r.at[0])
    o2s[0, 0] = (acc[xr, top] + o1r[0].astype(F32)).astype(BF16)
    send(("o2", "r", 0), o2s.at[0, 0], o2r.at[0, 0], dev(x=xr))
    got(("o1", "l"), o1r.at[1])
    o2s[1, 1] = (acc[xl, low] + o1r[1].astype(F32)).astype(BF16)
    send(("o2", "l", 1), o2s.at[1, 1], o2r.at[1, 1], dev(x=xl))
    products(1, x)
    for w, way in ((0, "r"), (1, "l")):
        for h in (1 - w, w):
            got(("o2", way, h), o2r.at[w, h])
    for h in range(2):
        rows = pl.ds(h * HALF, HALF)
        total = acc[x, rows] + o2r[0, h].astype(F32) + o2r[1, h].astype(F32)
        out_ref[rows, :] = total * FACTOR

    for cp in sent:
        cp.wait_send()

    @pl.when(jnp.logical_not(lone))
    def _():
        swap_copy.wait_send()

    assert len(keys) <= NSEM


def shards(out_grads, inputs, basis_grads, basis_inputs, counts):
    vmem = pl.BlockSpec(memory_space=pltpu.VMEM)
    hbm = pl.BlockSpec(memory_space=pl.ANY)
    return pl.pallas_call(
        kernel,
        out_shape=jax.ShapeDtypeStruct((COLS, WIDE), F32),
        in_specs=[hbm, hbm, hbm, hbm, pl.BlockSpec(memory_space=pltpu.SMEM)],
        out_specs=vmem,
        scratch_shapes=[
            pltpu.VMEM((UNITS, NX * QUARTER), BF16),
            pltpu.VMEM((NX, 32, QUARTER), BF16),
            pltpu.VMEM((2, NX, 32, QUARTER), BF16),
            pltpu.VMEM((CHUNKS, SLOTS, GROUP, TW), BF16),
            pltpu.VMEM((NX, COLS, BLOCK), BF16),
            pltpu.VMEM((COLS, BLOCK), BF16),
            pltpu.VMEM((NX, COLS, 8 * GROUP), BF16),
            pltpu.VMEM((TOK, DEPTH), BF16),
            pltpu.VMEM((FEATS, DEPTH), BF16),
            pltpu.VMEM((FEATS, TOK), BF16),
            pltpu.VMEM((SLOTS, FEATS, TOK), BF16),
            pltpu.VMEM((CHUNKS, 2, NX, HALF, TW), F32),
            pltpu.VMEM((CHUNKS, NX, HALF, TW), F32),
            pltpu.VMEM((CHUNKS, NX, HALF, TW), BF16),
            pltpu.VMEM((CHUNKS, 3, HALF, TW), BF16),
            pltpu.VMEM((CHUNKS, NH, NC, HALF, TW), BF16),
            pltpu.VMEM((NX, COLS, WIDE), F32),
            pltpu.VMEM((2, HALF, WIDE), BF16),
            pltpu.VMEM((2, HALF, WIDE), BF16),
            pltpu.VMEM((2, 2, HALF, WIDE), BF16),
            pltpu.VMEM((2, 2, HALF, WIDE), BF16),
            pltpu.SemaphoreType.DMA((NSEM,)),
            pltpu.SemaphoreType.DMA((NSEM,)),
            pltpu.SemaphoreType.DMA((5,)),
        ],
        compiler_params=pltpu.CompilerParams(
            collective_id=0, has_side_effects=True, vmem_limit_bytes=56 * 1024 * 1024
        ),
        cost_estimate=pl.CostEstimate(
            flops=2_200_000_000, bytes_accessed=10_000_000, transcendentals=0
        ),
    )(out_grads, basis_grads.T, inputs, basis_inputs.T, counts)


def solution(mesh):
    placed = (P(("dp", "basis"), None), P("dp", None), P("dp", "basis"), P(None, "basis"), P("dp"))
    return jax.shard_map(
        shards, mesh=mesh, in_specs=placed, out_specs=P("basis", "dp"), check_vma=False
    )
```

```python
import jax
import jax.numpy as jnp
from jax import lax
from jax.experimental import pallas as pl
from jax.experimental.pallas import tpu as pltpu
from jax.sharding import PartitionSpec as P

MESH = pl.DeviceIdType.MESH
BF16, F32 = jnp.bfloat16, jnp.float32

NX, NL, NZ, NH, NC = 4, 2, 12, 4, 2
SLOTS = NL * NZ
UNITS = 20
GROUP = NX * UNITS
BLOCK = SLOTS * GROUP
COLS = 160
HALF = COLS // 2
QUARTER = 512
CHUNKS = 2
TW = QUARTER // CHUNKS
SLOT = 128
FEATS = 64
WIDE = NZ * FEATS
TOK = 256
DEPTH = 6144
FACTOR = 1.0 / 2048.0
NSEM = 192


def dot(a, b, dims=((1,), (0,))):
    return lax.dot_general(a, b, (dims, ((), ())), preferred_element_type=F32)


def kernel(
    g_ref, b_ref, in_ref, bi_ref, cnt_ref, out_ref,
    gv, gs, ga, gb, bb, bv, picks, iv, biv, rt, rb, cb, cr, ss, sr, ab, acc, o1s, o1r, o2s, o2r,
    ssem, rsem, lsem,
):
    d, b = lax.axis_index("dp"), lax.axis_index("basis")
    yh, c = d // NC, d % NC
    x, yl, z = b // SLOTS, (b // NZ) % NL, b % NZ
    slot = yl * NZ + z

    def dev(yh=yh, c=c, x=x, yl=yl, z=z):
        return (yh * NC + c, x * SLOTS + yl * NZ + z)

    zr, zl = lax.rem(z + 1, NZ), lax.rem(z + NZ - 1, NZ)
    xr, xl, xo = lax.rem(x + 1, NX), lax.rem(x + 3, NX), lax.rem(x + 2, NX)
    yhs = [lax.rem(yh + r, NH) for r in range(NH)]
    pair_y, pair_c = dev(yl=1 - yl), dev(c=1 - c)
    right, left = dev(z=zr), dev(z=zl)
    swap = dev(yh=x, c=yl, x=yh, yl=c)
    swap_to = dev(yh=x, c=yl, x=yh, yl=1 - c)
    swap_from = dev(yh=x, c=1 - yl, x=yh, yl=c)
    lone = jnp.logical_and(yh == x, c == yl)

    barrier = pltpu.get_barrier_semaphore()
    peers = [right, left, pair_y, pair_c]
    peers += [dev(x=n, yl=m) for n in (xr, xl, xo) for m in (yl, 1 - yl)]
    peers += [dev(yh=yhs[r]) for r in (1, 2, 3)]
    peers += [swap_from]
    for peer in peers:
        pl.semaphore_signal(barrier, inc=1, device_id=peer, device_id_type=MESH)

    @pl.when(jnp.logical_not(lone))
    def _():
        pl.semaphore_signal(barrier, inc=1, device_id=swap, device_id_type=MESH)

    keys = {}
    sent = []

    def copy(key, src, dst, target):
        i = keys.setdefault(key, len(keys))
        return pltpu.make_async_remote_copy(
            src_ref=src, dst_ref=dst, send_sem=ssem.at[i], recv_sem=rsem.at[i],
            device_id=target, device_id_type=MESH,
        )

    def send(key, src, dst, target):
        cp = copy(key, src, dst, target)
        cp.start()
        sent.append(cp)

    def got(key, ref):
        copy(key, ref, ref, pair_c).wait_recv()

    load_in = pltpu.make_async_copy(in_ref, iv, lsem.at[0])
    load_bi = pltpu.make_async_copy(bi_ref, biv, lsem.at[1])
    load_g = pltpu.make_async_copy(g_ref, gv, lsem.at[2])
    load_b = pltpu.make_async_copy(b_ref, bv, lsem.at[3])
    for load in (load_g, load_b, load_bi, load_in):
        load.start()

    gs[...] = jnp.zeros_like(gs)
    load_g.wait()
    for q in range(NX):
        gs[q, 0:UNITS, :] = gv[:, q * QUARTER : (q + 1) * QUARTER]

    pl.semaphore_wait(barrier, jnp.where(lone, len(peers), len(peers) + 1))

    for n, xt in enumerate((xr, xl, xo)):
        send(("a", n, 0), gs.at[xt], ga.at[0, x], dev(x=xt))
        send(("a", n, 1), gs.at[xt], ga.at[1, x], dev(x=xt, yl=1 - yl))
    send(("a", 3, 1), gs.at[x], ga.at[1, x], pair_y)
    ga[0, x] = gs[x]

    load_b.wait()
    row = lax.broadcasted_iota(jnp.int32, (COLS, 8 * GROUP), 0)
    lane = lax.broadcasted_iota(jnp.int32, (COLS, 8 * GROUP), 1)
    place = row + 60 * ((row * 3277) >> 16)
    for q in range(NX):
        picks[q] = jnp.where(lane == place + UNITS * q, 1.0, 0.0).astype(BF16)
    for part in range(3):
        total = None
        for q in range(NX):
            start = q * (BLOCK // NX) + part * COLS
            term = dot(bv[:, start : start + COLS], picks[q])
            total = term if total is None else total + term
        bb[x, :, part * 640 : (part + 1) * 640] = total.astype(BF16)
    for h in range(2):
        for way, half, xt in (("r", h, xr), ("l", 1 - h, xl)):
            ref = bb.at[x, pl.ds(half * HALF, HALF)]
            send(("b", way, half), ref, ref, dev(x=xt))

    class Item:
        def __init__(self, name, ref, both, far):
            self.name, self.ref, self.both, self.far = name, ref, both, far

        def at(self, mine, shift):
            col = yl if mine else 1 - yl
            return self.ref(col * NZ + lax.rem(z + shift + 2 * NZ, NZ))

        def hop(self, way, mine, k, shift):
            ref = self.at(mine, shift)
            send((self.name, way, mine, k), ref, ref, right if way == "r" else left)

        def across(self, shift):
            ref = self.at(True, shift)
            send((self.name, "y", shift), ref, ref, pair_y)

        def last(self, way, mine):
            return 6 if (way == self.far) == mine else 5

        def begin(self, mine):
            if mine or self.both:
                self.hop("r", mine, 1, 0)
                self.hop("l", mine, 1, 0)

        def step(self, k):
            for mine in (True, False) if self.both else (True,):
                for way, sign in (("r", -1), ("l", 1)):
                    if k <= self.last(way, mine):
                        got((self.name, way, mine, k), self.at(mine, sign * k))
                        if k < self.last(way, mine):
                            self.hop(way, mine, k + 1, sign * k)
                        if not self.both:
                            self.across(sign * k)

        def end(self):
            if not self.both:
                shifts = []
                for k in range(1, 7):
                    shifts += [s * k for w, s in (("r", -1), ("l", 1)) if k <= self.last(w, True)]
                for shift in shifts:
                    got((self.name, "y", shift), self.at(False, shift))

    grads = [
        Item("g0", lambda s: gb.at[0, s], False, "r"),
        Item("g1", lambda s: gb.at[1, s], True, "r"),
    ]
    rot = Item("r", lambda s: rb.at[s], True, "l")

    for n, xt in enumerate((xl, xr, xo)):
        got(("a", n, 0), ga.at[0, xt])
        got(("a", n, 1), ga.at[1, xt])
    got(("a", 3, 1), ga.at[1, x])
    prow = lax.broadcasted_iota(jnp.int32, (GROUP, NX * 32), 0)
    plane = lax.broadcasted_iota(jnp.int32, (GROUP, NX * 32), 1)
    unit = plane & 31
    hit = jnp.logical_and(prow == (plane >> 5) * UNITS + unit, unit < UNITS)
    pick = jnp.where(hit, 1.0, 0.0).astype(BF16)
    for side, where in ((0, slot), (1, (1 - yl) * NZ + z)):
        packed = dot(pick, ga[side].reshape(NX * 32, QUARTER)).astype(BF16)
        for ch in range(CHUNKS):
            gb[ch, where] = packed[:, ch * TW : (ch + 1) * TW]
            grads[ch].begin(side == 0)

    load_bi.wait()
    load_in.wait()

    def slab(i, total):
        at = pl.ds(pl.multiple_of(i * 1536, 1536), 1536)
        return total + dot(iv[:, at], biv[:, at], ((1,), (1,)))

    tile = lax.fori_loop(0, DEPTH // 1536, slab, jnp.zeros((TOK, FEATS), F32))
    token = lax.broadcasted_iota(jnp.int32, (TOK, FEATS), 0)
    live = jnp.where(token < SLOT, cnt_ref[0], cnt_ref[1])
    tile = jnp.where((token & (SLOT - 1)) < live, tile, 0.0)
    rt[...] = tile.T.astype(BF16)
    own_copy = pltpu.make_async_copy(rt, rb.at[slot], lsem.at[4])

    swap_copy = copy(("swap",), rt, rb.at[c * NZ + z], swap)

    send(("swap", 2), rt, rb.at[c * NZ + z], swap_to)

    @pl.when(lone)
    def _():
        own_copy.start()
        own_copy.wait()

    @pl.when(jnp.logical_not(lone))
    def _():
        swap_copy.start()

    def rot_begin():
        @pl.when(jnp.logical_not(lone))
        def _():
            got(("swap",), rb.at[slot])

        rot.begin(True)
        got(("swap", 2), rot.at(False, 0))
        rot.begin(False)

    top, low = pl.ds(0, HALF), pl.ds(HALF, HALF)
    for it in range(1, 7):
        for item in grads:
            item.step(it)
        if it == 3:
            rot_begin()
        if it >= 4:
            rot.step(it - 3)
        if it == 3:
            got(("b", "r", 0), bb.at[xl, top])
            send(("b", "rr"), bb.at[xl, top], bb.at[xl, top], dev(x=xr))
            got(("b", "l", 1), bb.at[xr, low])
            send(("b", "ll"), bb.at[xr, low], bb.at[xr, low], dev(x=xl))
        if it == 5:
            got(("b", "l", 0), bb.at[xr, top])
            got(("b", "r", 1), bb.at[xl, low])
    grads[0].end()
    got(("b", "rr"), bb.at[xo, pl.ds(0, HALF)])
    got(("b", "ll"), bb.at[xo, pl.ds(HALF, HALF)])

    blocks = (xo, xr, xl, x)

    def multiply(i):
        for ch in range(CHUNKS):
            part = dot(bb[blocks[i]], gb[ch].reshape(BLOCK, TW))
            for e in range(TW // SLOT):
                for h in range(2):
                    at = slice(e * SLOT, (e + 1) * SLOT)
                    cb[i, h, ch * (TW // SLOT) + e] = part[h * HALF : (h + 1) * HALF, at]
        send(("c", i), cb.at[i, 1 - c], cr.at[i], pair_c)

    def scatter(i):
        got(("c", i), cr.at[i])
        for e in range(NH):
            ss[i, e] = (cb[i, c, e] + cr[i, e]).astype(BF16)
        for r in (2, 1, 3):
            send(("s", i, r), ss.at[i, yhs[r]], sr.at[i, r - 1], dev(yh=yhs[r]))

    def spread(i):
        total = cb[i, c, yh] + cr[i, yh]
        for r in (1, 3, 2):
            got(("s", i, r), sr.at[i, r - 1])
            total = total + sr[i, r - 1].astype(F32)
        ab[i, c, yh] = total.astype(BF16)
        mine = ab.at[i, c, yh]
        for r in (2, 1, 3):
            send(("t", i, r), mine, mine, dev(yh=yhs[r]))
        send(("u", i, 0), mine, mine, pair_c)

    def collect(i):
        for r in (1, 3, 2):
            ref = ab.at[i, c, yhs[NH - r]]
            got(("t", i, r), ref)
            send(("u", i, r), ref, ref, pair_c)

    def products(i):
        for r in range(NH):
            got(("u", i, r), ab.at[i, 1 - c, yhs[(NH - r) % NH]])
        for h in range(2):
            for f in range(3):
                total = None
                for e in range(NH):
                    first = (e // 2) * NZ + f * 4
                    at = slice((e % 2) * SLOT, (e % 2 + 1) * SLOT)
                    rows = rb[first : first + 4, :, at].reshape(4 * FEATS, SLOT)
                    term = dot(ab[i, h, e], rows, ((1,), (1,)))
                    total = term * term if total is None else total + term * term
                acc[i, pl.ds(h * HALF, HALF), pl.ds(f * 256, 256)] = total

    multiply(0)
    multiply(1)
    scatter(0)
    rot.step(4)
    multiply(2)
    scatter(1)
    multiply(3)
    scatter(2)
    spread(0)
    rot.step(5)
    scatter(3)
    spread(1)
    rot.step(6)
    collect(0)
    spread(2)
    products(0)
    o1s[0] = acc[0, top].astype(BF16)
    send(("o1", "r"), o1s.at[0], o1r.at[0], dev(x=xr))
    o1s[1] = acc[0, low].astype(BF16)
    send(("o1", "l"), o1s.at[1], o1r.at[1], dev(x=xl))
    collect(1)
    spread(3)
    products(1)
    o2s[0, 1] = acc[1, low].astype(BF16)
    send(("o2", "r", 1), o2s.at[0, 1], o2r.at[0, 1], dev(x=xr))
    collect(2)
    products(2)
    o2s[1, 0] = acc[2, top].astype(BF16)
    send(("o2", "l", 0), o2s.at[1, 0], o2r.at[1, 0], dev(x=xl))
    got(("o1", "r"), o1r.at[0])
    o2s[0, 0] = (acc[1, top] + o1r[0].astype(F32)).astype(BF16)
    send(("o2", "r", 0), o2s.at[0, 0], o2r.at[0, 0], dev(x=xr))
    got(("o1", "l"), o1r.at[1])
    o2s[1, 1] = (acc[2, low] + o1r[1].astype(F32)).astype(BF16)
    send(("o2", "l", 1), o2s.at[1, 1], o2r.at[1, 1], dev(x=xl))
    collect(3)
    products(3)
    for w, way in ((0, "r"), (1, "l")):
        for h in (1 - w, w):
            got(("o2", way, h), o2r.at[w, h])
    for h in range(2):
        rows = pl.ds(h * HALF, HALF)
        total = acc[3, rows] + o2r[0, h].astype(F32) + o2r[1, h].astype(F32)
        out_ref[rows, :] = total * FACTOR

    for cp in sent:
        cp.wait_send()

    @pl.when(jnp.logical_not(lone))
    def _():
        swap_copy.wait_send()

    assert len(keys) <= NSEM


def shards(out_grads, inputs, basis_grads, basis_inputs, counts):
    vmem = pl.BlockSpec(memory_space=pltpu.VMEM)
    hbm = pl.BlockSpec(memory_space=pl.ANY)
    return pl.pallas_call(
        kernel,
        out_shape=jax.ShapeDtypeStruct((COLS, WIDE), F32),
        in_specs=[hbm, hbm, hbm, hbm, pl.BlockSpec(memory_space=pltpu.SMEM)],
        out_specs=vmem,
        scratch_shapes=[
            pltpu.VMEM((UNITS, NX * QUARTER), BF16),
            pltpu.VMEM((NX, 32, QUARTER), BF16),
            pltpu.VMEM((2, NX, 32, QUARTER), BF16),
            pltpu.VMEM((CHUNKS, SLOTS, GROUP, TW), BF16),
            pltpu.VMEM((NX, COLS, BLOCK), BF16),
            pltpu.VMEM((COLS, BLOCK), BF16),
            pltpu.VMEM((NX, COLS, 8 * GROUP), BF16),
            pltpu.VMEM((TOK, DEPTH), BF16),
            pltpu.VMEM((FEATS, DEPTH), BF16),
            pltpu.VMEM((FEATS, TOK), BF16),
            pltpu.VMEM((SLOTS, FEATS, TOK), BF16),
            pltpu.VMEM((NX, NC, NH, HALF, SLOT), F32),
            pltpu.VMEM((NX, NH, HALF, SLOT), F32),
            pltpu.VMEM((NX, NH, HALF, SLOT), BF16),
            pltpu.VMEM((NX, 3, HALF, SLOT), BF16),
            pltpu.VMEM((NX, NC, NH, HALF, SLOT), BF16),
            pltpu.VMEM((NX, COLS, WIDE), F32),
            pltpu.VMEM((2, HALF, WIDE), BF16),
            pltpu.VMEM((2, HALF, WIDE), BF16),
            pltpu.VMEM((2, 2, HALF, WIDE), BF16),
            pltpu.VMEM((2, 2, HALF, WIDE), BF16),
            pltpu.SemaphoreType.DMA((NSEM,)),
            pltpu.SemaphoreType.DMA((NSEM,)),
            pltpu.SemaphoreType.DMA((5,)),
        ],
        compiler_params=pltpu.CompilerParams(
            collective_id=0, has_side_effects=True, vmem_limit_bytes=56 * 1024 * 1024
        ),
        cost_estimate=pl.CostEstimate(
            flops=2_200_000_000, bytes_accessed=10_000_000, transcendentals=0
        ),
    )(out_grads, basis_grads.T, inputs, basis_inputs.T, counts)


def solution(mesh):
    placed = (P(("dp", "basis"), None), P("dp", None), P("dp", "basis"), P(None, "basis"), P("dp"))
    return jax.shard_map(
        shards, mesh=mesh, in_specs=placed, out_specs=P("basis", "dp"), check_vma=False
    )
```

```python
import jax
import jax.numpy as jnp
from jax import lax
from jax.experimental import pallas as pl
from jax.experimental.pallas import tpu as pltpu
from jax.sharding import PartitionSpec as P

MESH = pl.DeviceIdType.MESH
BF16, F32 = jnp.bfloat16, jnp.float32

NX, NL, NZ, NH, NC = 4, 2, 12, 4, 2
SLOTS = NL * NZ
UNITS = 20
GROUP = NX * UNITS
BLOCK = SLOTS * GROUP
COLS = 160
HALF = COLS // 2
QUARTER = 512
CHUNKS = 4
TW = QUARTER // CHUNKS
PAIR = 2 * TW
SLOT = 128
FEATS = 64
WIDE = NZ * FEATS
TOK = 256
DEPTH = 6144
FACTOR = 1.0 / 2048.0
NSEM = 256


def dot(a, b, dims=((1,), (0,))):
    return lax.dot_general(a, b, (dims, ((), ())), preferred_element_type=F32)


def kernel(
    g_ref, b_ref, in_ref, bi_ref, cnt_ref, out_ref,
    gv, gs, ga, go, gb, bb, bv, picks, iv, biv, rt, rb, cb, cr, ss, sr, ab, acc, o1s, o1r, o2s, o2r,
    ssem, rsem, lsem,
):
    d, b = lax.axis_index("dp"), lax.axis_index("basis")
    yh, c = d // NC, d % NC
    x, yl, z = b // SLOTS, (b // NZ) % NL, b % NZ
    slot = yl * NZ + z

    def dev(yh=yh, c=c, x=x, yl=yl, z=z):
        return (yh * NC + c, x * SLOTS + yl * NZ + z)

    zr, zl = lax.rem(z + 1, NZ), lax.rem(z + NZ - 1, NZ)
    xr, xl, xo = lax.rem(x + 1, NX), lax.rem(x + 3, NX), lax.rem(x + 2, NX)
    yhs = [lax.rem(yh + r, NH) for r in range(NH)]
    pair_y, pair_c = dev(yl=1 - yl), dev(c=1 - c)
    right, left = dev(z=zr), dev(z=zl)
    swap = dev(yh=x, c=yl, x=yh, yl=c)
    swap_to = dev(yh=x, c=yl, x=yh, yl=1 - c)
    swap_from = dev(yh=x, c=1 - yl, x=yh, yl=c)
    lone = jnp.logical_and(yh == x, c == yl)

    barrier = pltpu.get_barrier_semaphore()
    peers = [right, left, pair_y, pair_c]
    peers += [dev(x=n, yl=m) for n in (xr, xl, xo) for m in (yl, 1 - yl)]
    peers += [dev(yh=yhs[r]) for r in (1, 2, 3)]
    peers += [swap_from]
    for peer in peers:
        pl.semaphore_signal(barrier, inc=1, device_id=peer, device_id_type=MESH)

    @pl.when(jnp.logical_not(lone))
    def _():
        pl.semaphore_signal(barrier, inc=1, device_id=swap, device_id_type=MESH)

    keys = {}
    sent = []

    def copy(key, src, dst, target):
        i = keys.setdefault(key, len(keys))
        return pltpu.make_async_remote_copy(
            src_ref=src, dst_ref=dst, send_sem=ssem.at[i], recv_sem=rsem.at[i],
            device_id=target, device_id_type=MESH,
        )

    def send(key, src, dst, target):
        cp = copy(key, src, dst, target)
        cp.start()
        sent.append(cp)

    def got(key, ref):
        copy(key, ref, ref, pair_c).wait_recv()

    load_in = pltpu.make_async_copy(in_ref, iv, lsem.at[0])
    load_bi = pltpu.make_async_copy(bi_ref, biv, lsem.at[1])
    load_g = pltpu.make_async_copy(g_ref, gv, lsem.at[2])
    load_b = pltpu.make_async_copy(b_ref, bv, lsem.at[3])
    for load in (load_g, load_b, load_bi, load_in):
        load.start()

    gs[...] = jnp.zeros_like(gs)
    load_g.wait()
    for q in range(NX):
        for h in range(2):
            start = q * QUARTER + h * PAIR
            gs[q, h, 0:UNITS, :] = gv[:, start : start + PAIR]

    pl.semaphore_wait(barrier, jnp.where(lone, len(peers), len(peers) + 1))

    for n, xt in enumerate((xr, xl, xo)):
        send(("a", n, 0), gs.at[xt], ga.at[x], dev(x=xt))
        send(("a", n, 1), gs.at[xt, 1], go.at[x], dev(x=xt, yl=1 - yl))
    send(("a", 3, 1), gs.at[x, 1], go.at[x], pair_y)
    ga[x] = gs[x]

    load_b.wait()
    row = lax.broadcasted_iota(jnp.int32, (COLS, 8 * GROUP), 0)
    lane = lax.broadcasted_iota(jnp.int32, (COLS, 8 * GROUP), 1)
    place = row + 60 * ((row * 3277) >> 16)
    for q in range(NX):
        picks[q] = jnp.where(lane == place + UNITS * q, 1.0, 0.0).astype(BF16)
    for part in range(3):
        total = None
        for q in range(NX):
            start = q * (BLOCK // NX) + part * COLS
            term = dot(bv[:, start : start + COLS], picks[q])
            total = term if total is None else total + term
        bb[x, :, part * 640 : (part + 1) * 640] = total.astype(BF16)
    for h in range(2):
        for way, half, xt in (("r", h, xr), ("l", 1 - h, xl)):
            ref = bb.at[x, pl.ds(half * HALF, HALF)]
            send(("b", way, half), ref, ref, dev(x=xt))

    class Item:
        def __init__(self, name, ref, both, far):
            self.name, self.ref, self.both, self.far = name, ref, both, far

        def at(self, mine, shift):
            col = yl if mine else 1 - yl
            return self.ref(col * NZ + lax.rem(z + shift + 2 * NZ, NZ))

        def hop(self, way, mine, k, shift):
            ref = self.at(mine, shift)
            send((self.name, way, mine, k), ref, ref, right if way == "r" else left)

        def across(self, shift):
            ref = self.at(True, shift)
            send((self.name, "y", shift), ref, ref, pair_y)

        def last(self, way, mine):
            return 6 if (way == self.far) == mine else 5

        def begin(self, mine):
            if mine or self.both:
                self.hop("r", mine, 1, 0)
                self.hop("l", mine, 1, 0)

        def step(self, k):
            for mine in (True, False) if self.both else (True,):
                for way, sign in (("r", -1), ("l", 1)):
                    if k <= self.last(way, mine):
                        got((self.name, way, mine, k), self.at(mine, sign * k))
                        if k < self.last(way, mine):
                            self.hop(way, mine, k + 1, sign * k)
                        if not self.both:
                            self.across(sign * k)

        def end(self):
            if not self.both:
                shifts = [0]
                for k in range(1, 7):
                    shifts += [s * k for w, s in (("r", -1), ("l", 1)) if k <= self.last(w, True)]
                for shift in shifts:
                    got((self.name, "y", shift), self.at(False, shift))

    grads = [
        Item("g0", lambda s: gb.at[0, s], False, "r"),
        Item("g1", lambda s: gb.at[1, s], False, "l"),
        Item("g2", lambda s: gb.at[2, s], True, "r"),
        Item("g3", lambda s: gb.at[3, s], True, "l"),
    ]
    rot = Item("r", lambda s: rb.at[s], True, "l")

    for n, xt in enumerate((xl, xr, xo)):
        got(("a", n, 0), ga.at[xt])
    prow = lax.broadcasted_iota(jnp.int32, (GROUP, NX * 32), 0)
    plane = lax.broadcasted_iota(jnp.int32, (GROUP, NX * 32), 1)
    unit = plane & 31
    hit = jnp.logical_and(prow == (plane >> 5) * UNITS + unit, unit < UNITS)
    pick = jnp.where(hit, 1.0, 0.0).astype(BF16)
    for h in range(2):
        packed = dot(pick, ga[:, h].reshape(NX * 32, PAIR)).astype(BF16)
        for ch in (2 * h, 2 * h + 1):
            gb[ch, slot] = packed[:, (ch % 2) * TW : (ch % 2 + 1) * TW]
            grads[ch].begin(True)
            if not grads[ch].both:
                grads[ch].across(0)
    for n, xt in enumerate((xl, xr, xo, x)):
        got(("a", n, 1), go.at[xt])
    packed = dot(pick, go[...].reshape(NX * 32, PAIR)).astype(BF16)
    for ch in (2, 3):
        gb[ch, (1 - yl) * NZ + z] = packed[:, (ch % 2) * TW : (ch % 2 + 1) * TW]
        grads[ch].begin(False)

    load_bi.wait()
    load_in.wait()

    def slab(i, total):
        at = pl.ds(pl.multiple_of(i * 1536, 1536), 1536)
        return total + dot(iv[:, at], biv[:, at], ((1,), (1,)))

    tile = lax.fori_loop(0, DEPTH // 1536, slab, jnp.zeros((TOK, FEATS), F32))
    token = lax.broadcasted_iota(jnp.int32, (TOK, FEATS), 0)
    live = jnp.where(token < SLOT, cnt_ref[0], cnt_ref[1])
    tile = jnp.where((token & (SLOT - 1)) < live, tile, 0.0)
    rt[...] = tile.T.astype(BF16)
    own_copy = pltpu.make_async_copy(rt, rb.at[slot], lsem.at[4])

    swap_copy = copy(("swap",), rt, rb.at[c * NZ + z], swap)

    send(("swap", 2), rt, rb.at[c * NZ + z], swap_to)

    @pl.when(lone)
    def _():
        own_copy.start()
        own_copy.wait()

    @pl.when(jnp.logical_not(lone))
    def _():
        swap_copy.start()

    def rot_begin():
        @pl.when(jnp.logical_not(lone))
        def _():
            got(("swap",), rb.at[slot])

        rot.begin(True)
        got(("swap", 2), rot.at(False, 0))
        rot.begin(False)

    top, low = pl.ds(0, HALF), pl.ds(HALF, HALF)
    for it in range(1, 7):
        for item in grads:
            item.step(it)
        if it == 4:
            rot_begin()
        if it >= 5:
            rot.step(it - 4)
        if it == 3:
            got(("b", "r", 0), bb.at[xl, top])
            send(("b", "rr"), bb.at[xl, top], bb.at[xl, top], dev(x=xr))
            got(("b", "l", 1), bb.at[xr, low])
            send(("b", "ll"), bb.at[xr, low], bb.at[xr, low], dev(x=xl))
        if it == 5:
            got(("b", "l", 0), bb.at[xr, top])
            got(("b", "r", 1), bb.at[xl, low])
    grads[0].end()
    grads[1].end()
    got(("b", "rr"), bb.at[xo, pl.ds(0, HALF)])
    got(("b", "ll"), bb.at[xo, pl.ds(HALF, HALF)])

    blocks = (xo, xr, xl, x)

    def multiply(i):
        for ch in range(0, CHUNKS, 2):
            both = [gb[ch + e].reshape(BLOCK, TW) for e in range(2)]
            part = dot(bb[blocks[i]], jnp.concatenate(both, axis=1))
            for e in range(2):
                for h in range(2):
                    at = slice(e * SLOT, (e + 1) * SLOT)
                    cb[i, h, ch + e] = part[h * HALF : (h + 1) * HALF, at]
        send(("c", i), cb.at[i, 1 - c], cr.at[i], pair_c)

    def scatter(i):
        got(("c", i), cr.at[i])
        for e in range(NH):
            ss[i, e] = (cb[i, c, e] + cr[i, e]).astype(BF16)
        for r in (2, 1, 3):
            send(("s", i, r), ss.at[i, yhs[r]], sr.at[i, r - 1], dev(yh=yhs[r]))

    def spread(i):
        total = cb[i, c, yh] + cr[i, yh]
        for r in (1, 3, 2):
            got(("s", i, r), sr.at[i, r - 1])
            total = total + sr[i, r - 1].astype(F32)
        ab[i, c, yh] = total.astype(BF16)
        mine = ab.at[i, c, yh]
        for r in (2, 1, 3):
            send(("t", i, r), mine, mine, dev(yh=yhs[r]))
        send(("u", i, 0), mine, mine, pair_c)

    def collect(i):
        for r in (1, 3, 2):
            ref = ab.at[i, c, yhs[NH - r]]
            got(("t", i, r), ref)
            send(("u", i, r), ref, ref, pair_c)

    def products(i):
        for r in range(NH):
            got(("u", i, r), ab.at[i, 1 - c, yhs[(NH - r) % NH]])
        for h in range(2):
            for f in range(3):
                total = None
                for e in range(NH):
                    first = (e // 2) * NZ + f * 4
                    at = slice((e % 2) * SLOT, (e % 2 + 1) * SLOT)
                    rows = rb[first : first + 4, :, at].reshape(4 * FEATS, SLOT)
                    term = dot(ab[i, h, e], rows, ((1,), (1,)))
                    total = term * term if total is None else total + term * term
                acc[i, pl.ds(h * HALF, HALF), pl.ds(f * 256, 256)] = total

    multiply(0)
    multiply(1)
    scatter(0)
    rot.step(3)
    multiply(2)
    scatter(1)
    multiply(3)
    scatter(2)
    spread(0)
    rot.step(4)
    scatter(3)
    spread(1)
    rot.step(5)
    collect(0)
    spread(2)
    rot.step(6)
    products(0)
    o1s[0] = acc[0, top].astype(BF16)
    send(("o1", "r"), o1s.at[0], o1r.at[0], dev(x=xr))
    o1s[1] = acc[0, low].astype(BF16)
    send(("o1", "l"), o1s.at[1], o1r.at[1], dev(x=xl))
    collect(1)
    spread(3)
    products(1)
    o2s[0, 1] = acc[1, low].astype(BF16)
    send(("o2", "r", 1), o2s.at[0, 1], o2r.at[0, 1], dev(x=xr))
    collect(2)
    products(2)
    o2s[1, 0] = acc[2, top].astype(BF16)
    send(("o2", "l", 0), o2s.at[1, 0], o2r.at[1, 0], dev(x=xl))
    got(("o1", "r"), o1r.at[0])
    o2s[0, 0] = (acc[1, top] + o1r[0].astype(F32)).astype(BF16)
    send(("o2", "r", 0), o2s.at[0, 0], o2r.at[0, 0], dev(x=xr))
    got(("o1", "l"), o1r.at[1])
    o2s[1, 1] = (acc[2, low] + o1r[1].astype(F32)).astype(BF16)
    send(("o2", "l", 1), o2s.at[1, 1], o2r.at[1, 1], dev(x=xl))
    collect(3)
    products(3)
    for w, way in ((0, "r"), (1, "l")):
        for h in (1 - w, w):
            got(("o2", way, h), o2r.at[w, h])
    for h in range(2):
        rows = pl.ds(h * HALF, HALF)
        total = acc[3, rows] + o2r[0, h].astype(F32) + o2r[1, h].astype(F32)
        out_ref[rows, :] = total * FACTOR

    for cp in sent:
        cp.wait_send()

    @pl.when(jnp.logical_not(lone))
    def _():
        swap_copy.wait_send()

    assert len(keys) <= NSEM


def shards(out_grads, inputs, basis_grads, basis_inputs, counts):
    vmem = pl.BlockSpec(memory_space=pltpu.VMEM)
    hbm = pl.BlockSpec(memory_space=pl.ANY)
    return pl.pallas_call(
        kernel,
        out_shape=jax.ShapeDtypeStruct((COLS, WIDE), F32),
        in_specs=[hbm, hbm, hbm, hbm, pl.BlockSpec(memory_space=pltpu.SMEM)],
        out_specs=vmem,
        scratch_shapes=[
            pltpu.VMEM((UNITS, NX * QUARTER), BF16),
            pltpu.VMEM((NX, 2, 32, PAIR), BF16),
            pltpu.VMEM((NX, 2, 32, PAIR), BF16),
            pltpu.VMEM((NX, 32, PAIR), BF16),
            pltpu.VMEM((CHUNKS, SLOTS, GROUP, TW), BF16),
            pltpu.VMEM((NX, COLS, BLOCK), BF16),
            pltpu.VMEM((COLS, BLOCK), BF16),
            pltpu.VMEM((NX, COLS, 8 * GROUP), BF16),
            pltpu.VMEM((TOK, DEPTH), BF16),
            pltpu.VMEM((FEATS, DEPTH), BF16),
            pltpu.VMEM((FEATS, TOK), BF16),
            pltpu.VMEM((SLOTS, FEATS, TOK), BF16),
            pltpu.VMEM((NX, NC, NH, HALF, SLOT), F32),
            pltpu.VMEM((NX, NH, HALF, SLOT), F32),
            pltpu.VMEM((NX, NH, HALF, SLOT), BF16),
            pltpu.VMEM((NX, 3, HALF, SLOT), BF16),
            pltpu.VMEM((NX, NC, NH, HALF, SLOT), BF16),
            pltpu.VMEM((NX, COLS, WIDE), F32),
            pltpu.VMEM((2, HALF, WIDE), BF16),
            pltpu.VMEM((2, HALF, WIDE), BF16),
            pltpu.VMEM((2, 2, HALF, WIDE), BF16),
            pltpu.VMEM((2, 2, HALF, WIDE), BF16),
            pltpu.SemaphoreType.DMA((NSEM,)),
            pltpu.SemaphoreType.DMA((NSEM,)),
            pltpu.SemaphoreType.DMA((5,)),
        ],
        compiler_params=pltpu.CompilerParams(
            collective_id=0, has_side_effects=True, vmem_limit_bytes=56 * 1024 * 1024
        ),
        cost_estimate=pl.CostEstimate(
            flops=2_200_000_000, bytes_accessed=10_000_000, transcendentals=0
        ),
    )(out_grads, basis_grads.T, inputs, basis_inputs.T, counts)


def solution(mesh):
    placed = (P(("dp", "basis"), None), P("dp", None), P("dp", "basis"), P(None, "basis"), P("dp"))
    return jax.shard_map(
        shards, mesh=mesh, in_specs=placed, out_specs=P("basis", "dp"), check_vma=False
    )
```

```python
import jax
import jax.numpy as jnp
from jax import lax
from jax.experimental import pallas as pl
from jax.experimental.pallas import tpu as pltpu
from jax.sharding import PartitionSpec as P

MESH = pl.DeviceIdType.MESH
BF16, F32 = jnp.bfloat16, jnp.float32

NX, NL, NZ, NH, NC = 4, 2, 12, 4, 2
SLOTS = NL * NZ
UNITS = 20
GROUP = NX * UNITS
BLOCK = SLOTS * GROUP
COLS = 160
HALF = COLS // 2
QUARTER = 512
CHUNKS = 4
TW = QUARTER // CHUNKS
PAIR = 2 * TW
SLOT = 128
FEATS = 64
WIDE = NZ * FEATS
TOK = 256
DEPTH = 6144
FACTOR = 1.0 / 2048.0
NSEM = 256


def dot(a, b, dims=((1,), (0,))):
    return lax.dot_general(a, b, (dims, ((), ())), preferred_element_type=F32)


def kernel(
    g_ref, b_ref, in_ref, bi_ref, cnt_ref, out_ref,
    gs, ga, go, gb, bb, bv, picks, iv, biv, rt, rb, cb, cr, ss, sr, ab, acc, o1s, o1r, o2s, o2r,
    ssem, rsem, lsem,
):
    d, b = lax.axis_index("dp"), lax.axis_index("basis")
    yh, c = d // NC, d % NC
    x, yl, z = b // SLOTS, (b // NZ) % NL, b % NZ
    slot = yl * NZ + z

    def dev(yh=yh, c=c, x=x, yl=yl, z=z):
        return (yh * NC + c, x * SLOTS + yl * NZ + z)

    zr, zl = lax.rem(z + 1, NZ), lax.rem(z + NZ - 1, NZ)
    xr, xl, xo = lax.rem(x + 1, NX), lax.rem(x + 3, NX), lax.rem(x + 2, NX)
    yhs = [lax.rem(yh + r, NH) for r in range(NH)]
    pair_y, pair_c = dev(yl=1 - yl), dev(c=1 - c)
    right, left = dev(z=zr), dev(z=zl)
    swap = dev(yh=x, c=yl, x=yh, yl=c)
    swap_to = dev(yh=x, c=yl, x=yh, yl=1 - c)
    swap_from = dev(yh=x, c=1 - yl, x=yh, yl=c)
    lone = jnp.logical_and(yh == x, c == yl)

    barrier = pltpu.get_barrier_semaphore()
    peers = [right, left, pair_y, pair_c]
    peers += [dev(x=n, yl=m) for n in (xr, xl, xo) for m in (yl, 1 - yl)]
    peers += [dev(yh=yhs[r]) for r in (1, 2, 3)]
    peers += [swap_from]
    for peer in peers:
        pl.semaphore_signal(barrier, inc=1, device_id=peer, device_id_type=MESH)

    @pl.when(jnp.logical_not(lone))
    def _():
        pl.semaphore_signal(barrier, inc=1, device_id=swap, device_id_type=MESH)

    keys = {}
    sent = []

    def copy(key, src, dst, target):
        i = keys.setdefault(key, len(keys))
        return pltpu.make_async_remote_copy(
            src_ref=src, dst_ref=dst, send_sem=ssem.at[i], recv_sem=rsem.at[i],
            device_id=target, device_id_type=MESH,
        )

    def send(key, src, dst, target):
        cp = copy(key, src, dst, target)
        cp.start()
        sent.append(cp)

    def got(key, ref):
        copy(key, ref, ref, pair_c).wait_recv()

    load_in = pltpu.make_async_copy(in_ref, iv, lsem.at[0])
    load_bi = pltpu.make_async_copy(bi_ref, biv, lsem.at[1])
    load_b = pltpu.make_async_copy(b_ref, bv, lsem.at[3])
    for load in (load_b, load_bi, load_in):
        load.start()

    gs[...] = jnp.zeros_like(gs)
    for q in range(NX):
        for h in range(2):
            start = q * QUARTER + h * PAIR
            gs[q, h, 0:UNITS, :] = g_ref[:, start : start + PAIR]

    pl.semaphore_wait(barrier, jnp.where(lone, len(peers), len(peers) + 1))

    for n, xt in enumerate((xr, xl, xo)):
        send(("a", n, 0), gs.at[xt], ga.at[x], dev(x=xt))
        send(("a", n, 1), gs.at[xt, 1], go.at[x], dev(x=xt, yl=1 - yl))
    send(("a", 3, 1), gs.at[x, 1], go.at[x], pair_y)
    ga[x] = gs[x]

    load_b.wait()
    row = lax.broadcasted_iota(jnp.int32, (COLS, 8 * GROUP), 0)
    lane = lax.broadcasted_iota(jnp.int32, (COLS, 8 * GROUP), 1)
    place = row + 60 * ((row * 3277) >> 16)
    for q in range(NX):
        picks[q] = jnp.where(lane == place + UNITS * q, 1.0, 0.0).astype(BF16)
    for part in range(3):
        total = None
        for q in range(NX):
            start = q * (BLOCK // NX) + part * COLS
            term = dot(bv[:, start : start + COLS], picks[q])
            total = term if total is None else total + term
        bb[x, :, part * 640 : (part + 1) * 640] = total.astype(BF16)
    for h in range(2):
        for way, half, xt in (("r", h, xr), ("l", 1 - h, xl)):
            ref = bb.at[x, pl.ds(half * HALF, HALF)]
            send(("b", way, half), ref, ref, dev(x=xt))

    class Item:
        def __init__(self, name, ref, both, far):
            self.name, self.ref, self.both, self.far = name, ref, both, far

        def at(self, mine, shift):
            col = yl if mine else 1 - yl
            return self.ref(col * NZ + lax.rem(z + shift + 2 * NZ, NZ))

        def hop(self, way, mine, k, shift):
            ref = self.at(mine, shift)
            send((self.name, way, mine, k), ref, ref, right if way == "r" else left)

        def across(self, shift):
            ref = self.at(True, shift)
            send((self.name, "y", shift), ref, ref, pair_y)

        def last(self, way, mine):
            return 6 if (way == self.far) == mine else 5

        def begin(self, mine):
            if mine or self.both:
                self.hop("r", mine, 1, 0)
                self.hop("l", mine, 1, 0)

        def step(self, k):
            for mine in (True, False) if self.both else (True,):
                for way, sign in (("r", -1), ("l", 1)):
                    if k <= self.last(way, mine):
                        got((self.name, way, mine, k), self.at(mine, sign * k))
                        if k < self.last(way, mine):
                            self.hop(way, mine, k + 1, sign * k)
                        if not self.both:
                            self.across(sign * k)
            if not self.both and k >= 2:
                self.crossed(k - 2)

        def crossed(self, k):
            ways = [(w, g) for w, g in (("r", -1), ("l", 1)) if k <= self.last(w, True)]
            for shift in [g * k for w, g in ways] if k else [0]:
                got((self.name, "y", shift), self.at(False, shift))

        def end(self):
            self.crossed(5)
            self.crossed(6)

    grads = [
        Item("g0", lambda s: gb.at[0, s], False, "r"),
        Item("g1", lambda s: gb.at[1, s], False, "l"),
        Item("g2", lambda s: gb.at[2, s], True, "r"),
        Item("g3", lambda s: gb.at[3, s], True, "l"),
    ]
    rot = Item("r", lambda s: rb.at[s], True, "l")

    load_bi.wait()
    load_in.wait()

    def slab(i, total):
        at = pl.ds(pl.multiple_of(i * 1536, 1536), 1536)
        return total + dot(iv[:, at], biv[:, at], ((1,), (1,)))

    tile = lax.fori_loop(0, DEPTH // 1536, slab, jnp.zeros((TOK, FEATS), F32))
    token = lax.broadcasted_iota(jnp.int32, (TOK, FEATS), 0)
    live = jnp.where(token < SLOT, cnt_ref[0], cnt_ref[1])
    tile = jnp.where((token & (SLOT - 1)) < live, tile, 0.0)
    rt[...] = tile.T.astype(BF16)
    own_copy = pltpu.make_async_copy(rt, rb.at[slot], lsem.at[4])

    swap_copy = copy(("swap",), rt, rb.at[c * NZ + z], swap)

    send(("swap", 2), rt, rb.at[c * NZ + z], swap_to)

    @pl.when(lone)
    def _():
        own_copy.start()
        own_copy.wait()

    @pl.when(jnp.logical_not(lone))
    def _():
        swap_copy.start()

    for n, xt in enumerate((xl, xr, xo)):
        got(("a", n, 0), ga.at[xt])
    prow = lax.broadcasted_iota(jnp.int32, (GROUP, NX * 32), 0)
    plane = lax.broadcasted_iota(jnp.int32, (GROUP, NX * 32), 1)
    unit = plane & 31
    hit = jnp.logical_and(prow == (plane >> 5) * UNITS + unit, unit < UNITS)
    pick = jnp.where(hit, 1.0, 0.0).astype(BF16)
    for h in range(2):
        packed = dot(pick, ga[:, h].reshape(NX * 32, PAIR)).astype(BF16)
        for ch in (2 * h, 2 * h + 1):
            gb[ch, slot] = packed[:, (ch % 2) * TW : (ch % 2 + 1) * TW]
            grads[ch].begin(True)
            if not grads[ch].both:
                grads[ch].across(0)
    for n, xt in enumerate((xl, xr, xo, x)):
        got(("a", n, 1), go.at[xt])
    packed = dot(pick, go[...].reshape(NX * 32, PAIR)).astype(BF16)
    for ch in (2, 3):
        gb[ch, (1 - yl) * NZ + z] = packed[:, (ch % 2) * TW : (ch % 2 + 1) * TW]
        grads[ch].begin(False)

    def rot_begin():
        @pl.when(jnp.logical_not(lone))
        def _():
            got(("swap",), rb.at[slot])

        rot.begin(True)
        got(("swap", 2), rot.at(False, 0))
        rot.begin(False)

    top, low = pl.ds(0, HALF), pl.ds(HALF, HALF)
    for it in range(1, 7):
        for item in grads:
            item.step(it)
        if it == 3:
            rot_begin()
        if it >= 4:
            rot.step(it - 3)
        if it == 3:
            got(("b", "r", 0), bb.at[xl, top])
            send(("b", "rr"), bb.at[xl, top], bb.at[xl, top], dev(x=xr))
            got(("b", "l", 1), bb.at[xr, low])
            send(("b", "ll"), bb.at[xr, low], bb.at[xr, low], dev(x=xl))
        if it == 5:
            got(("b", "l", 0), bb.at[xr, top])
            got(("b", "r", 1), bb.at[xl, low])
    grads[0].end()
    grads[1].end()
    got(("b", "rr"), bb.at[xo, pl.ds(0, HALF)])
    got(("b", "ll"), bb.at[xo, pl.ds(HALF, HALF)])

    early = len(sent)

    blocks = (xo, xr, xl, x)

    def multiply(i):
        for ch in range(0, CHUNKS, 2):
            both = [gb[ch + e].reshape(BLOCK, TW) for e in range(2)]
            part = dot(bb[blocks[i]], jnp.concatenate(both, axis=1))
            for e in range(2):
                for h in range(2):
                    at = slice(e * SLOT, (e + 1) * SLOT)
                    cb[i, h, ch + e] = part[h * HALF : (h + 1) * HALF, at]
        send(("c", i), cb.at[i, 1 - c], cr.at[i], pair_c)

    def scatter(i):
        got(("c", i), cr.at[i])
        for e in range(NH):
            ss[i, e] = (cb[i, c, e] + cr[i, e]).astype(BF16)
        for r in (2, 1, 3):
            send(("s", i, r), ss.at[i, yhs[r]], sr.at[i, r - 1], dev(yh=yhs[r]))

    def spread(i):
        total = cb[i, c, yh] + cr[i, yh]
        for r in (1, 3, 2):
            got(("s", i, r), sr.at[i, r - 1])
            total = total + sr[i, r - 1].astype(F32)
        ab[i, c, yh] = total.astype(BF16)
        mine = ab.at[i, c, yh]
        for r in (2, 1, 3):
            send(("t", i, r), mine, mine, dev(yh=yhs[r]))
        send(("u", i, 0), mine, mine, pair_c)

    def collect(i):
        for r in (1, 3, 2):
            ref = ab.at[i, c, yhs[NH - r]]
            got(("t", i, r), ref)
            send(("u", i, r), ref, ref, pair_c)

    def products(i):
        for r in range(NH):
            got(("u", i, r), ab.at[i, 1 - c, yhs[(NH - r) % NH]])
        for h in range(2):
            for f in range(3):
                total = None
                for e in range(NH):
                    first = (e // 2) * NZ + f * 4
                    at = slice((e % 2) * SLOT, (e % 2 + 1) * SLOT)
                    rows = rb[first : first + 4, :, at].reshape(4 * FEATS, SLOT)
                    term = dot(ab[i, h, e], rows, ((1,), (1,)))
                    total = term * term if total is None else total + term * term
                acc[i, pl.ds(h * HALF, HALF), pl.ds(f * 256, 256)] = total

    multiply(0)
    multiply(1)
    scatter(0)
    multiply(2)
    scatter(1)
    multiply(3)
    scatter(2)
    spread(0)
    rot.step(4)
    scatter(3)
    spread(1)
    rot.step(5)
    collect(0)
    spread(2)
    rot.step(6)
    products(0)
    o1s[0] = acc[0, top].astype(BF16)
    send(("o1", "r"), o1s.at[0], o1r.at[0], dev(x=xr))
    o1s[1] = acc[0, low].astype(BF16)
    send(("o1", "l"), o1s.at[1], o1r.at[1], dev(x=xl))
    collect(1)
    spread(3)
    products(1)
    o2s[0, 1] = acc[1, low].astype(BF16)
    send(("o2", "r", 1), o2s.at[0, 1], o2r.at[0, 1], dev(x=xr))
    collect(2)
    products(2)
    o2s[1, 0] = acc[2, top].astype(BF16)
    send(("o2", "l", 0), o2s.at[1, 0], o2r.at[1, 0], dev(x=xl))
    for cp in sent[:early]:
        cp.wait_send()
    got(("o1", "r"), o1r.at[0])
    o2s[0, 0] = (acc[1, top] + o1r[0].astype(F32)).astype(BF16)
    send(("o2", "r", 0), o2s.at[0, 0], o2r.at[0, 0], dev(x=xr))
    got(("o1", "l"), o1r.at[1])
    o2s[1, 1] = (acc[2, low] + o1r[1].astype(F32)).astype(BF16)
    send(("o2", "l", 1), o2s.at[1, 1], o2r.at[1, 1], dev(x=xl))
    collect(3)
    for cp in sent[early : len(sent) - 8]:
        cp.wait_send()
    late = len(sent) - 8
    products(3)
    for w, way in ((0, "r"), (1, "l")):
        for h in (1 - w, w):
            got(("o2", way, h), o2r.at[w, h])
    for h in range(2):
        rows = pl.ds(h * HALF, HALF)
        total = acc[3, rows] + o2r[0, h].astype(F32) + o2r[1, h].astype(F32)
        out_ref[rows, :] = total * FACTOR

    for cp in sent[late:]:
        cp.wait_send()

    @pl.when(jnp.logical_not(lone))
    def _():
        swap_copy.wait_send()

    assert len(keys) <= NSEM


def shards(out_grads, inputs, basis_grads, basis_inputs, counts):
    vmem = pl.BlockSpec(memory_space=pltpu.VMEM)
    hbm = pl.BlockSpec(memory_space=pl.ANY)
    return pl.pallas_call(
        kernel,
        out_shape=jax.ShapeDtypeStruct((COLS, WIDE), F32),
        in_specs=[vmem, hbm, hbm, hbm, pl.BlockSpec(memory_space=pltpu.SMEM)],
        out_specs=vmem,
        scratch_shapes=[
            pltpu.VMEM((NX, 2, 32, PAIR), BF16),
            pltpu.VMEM((NX, 2, 32, PAIR), BF16),
            pltpu.VMEM((NX, 32, PAIR), BF16),
            pltpu.VMEM((CHUNKS, SLOTS, GROUP, TW), BF16),
            pltpu.VMEM((NX, COLS, BLOCK), BF16),
            pltpu.VMEM((COLS, BLOCK), BF16),
            pltpu.VMEM((NX, COLS, 8 * GROUP), BF16),
            pltpu.VMEM((TOK, DEPTH), BF16),
            pltpu.VMEM((FEATS, DEPTH), BF16),
            pltpu.VMEM((FEATS, TOK), BF16),
            pltpu.VMEM((SLOTS, FEATS, TOK), BF16),
            pltpu.VMEM((NX, NC, NH, HALF, SLOT), F32),
            pltpu.VMEM((NX, NH, HALF, SLOT), F32),
            pltpu.VMEM((NX, NH, HALF, SLOT), BF16),
            pltpu.VMEM((NX, 3, HALF, SLOT), BF16),
            pltpu.VMEM((NX, NC, NH, HALF, SLOT), BF16),
            pltpu.VMEM((NX, COLS, WIDE), F32),
            pltpu.VMEM((2, HALF, WIDE), BF16),
            pltpu.VMEM((2, HALF, WIDE), BF16),
            pltpu.VMEM((2, 2, HALF, WIDE), BF16),
            pltpu.VMEM((2, 2, HALF, WIDE), BF16),
            pltpu.SemaphoreType.DMA((NSEM,)),
            pltpu.SemaphoreType.DMA((NSEM,)),
            pltpu.SemaphoreType.DMA((5,)),
        ],
        compiler_params=pltpu.CompilerParams(
            collective_id=0, has_side_effects=True, vmem_limit_bytes=53 * 1024 * 1024
        ),
        cost_estimate=pl.CostEstimate(
            flops=2_200_000_000, bytes_accessed=10_000_000, transcendentals=0
        ),
    )(out_grads, basis_grads.T, inputs, basis_inputs.T, counts)


def solution(mesh):
    placed = (P(("dp", "basis"), None), P("dp", None), P("dp", "basis"), P(None, "basis"), P("dp"))
    return jax.shard_map(
        shards, mesh=mesh, in_specs=placed, out_specs=P("basis", "dp"), check_vma=False
    )
```

```python
import jax
import jax.numpy as jnp
from jax import lax
from jax.experimental import pallas as pl
from jax.experimental.pallas import tpu as pltpu
from jax.sharding import PartitionSpec as P

MESH = pl.DeviceIdType.MESH
BF16, F32 = jnp.bfloat16, jnp.float32

NX, NL, NZ, NH, NC = 4, 2, 12, 4, 2
SLOTS = NL * NZ
UNITS = 20
GROUP = NX * UNITS
BLOCK = SLOTS * GROUP
COLS = 160
HALF = COLS // 2
QUARTER = 512
CHUNKS = 4
TW = QUARTER // CHUNKS
PAIR = 2 * TW
SLOT = 128
FEATS = 64
WIDE = NZ * FEATS
TOK = 256
DEPTH = 6144
FACTOR = 1.0 / 2048.0
NSEM = 256


def dot(a, b, dims=((1,), (0,))):
    return lax.dot_general(a, b, (dims, ((), ())), preferred_element_type=F32)


def kernel(
    g_ref, b_ref, in_ref, bi_ref, cnt_ref, out_ref,
    gs, ga, go, gb, bb, bv, picks, iv, biv, rt, rb, cb, cr, ss, sr, ab, acc, o1s, o1r, o2s, o2r,
    ssem, rsem, lsem,
):
    d, b = lax.axis_index("dp"), lax.axis_index("basis")
    yh, c = d // NC, d % NC
    x, yl, z = b // SLOTS, (b // NZ) % NL, b % NZ
    slot = yl * NZ + z

    def dev(yh=yh, c=c, x=x, yl=yl, z=z):
        return (yh * NC + c, x * SLOTS + yl * NZ + z)

    zr, zl = lax.rem(z + 1, NZ), lax.rem(z + NZ - 1, NZ)
    xr, xl, xo = lax.rem(x + 1, NX), lax.rem(x + 3, NX), lax.rem(x + 2, NX)
    yhs = [lax.rem(yh + r, NH) for r in range(NH)]
    pair_y, pair_c = dev(yl=1 - yl), dev(c=1 - c)
    right, left = dev(z=zr), dev(z=zl)
    swap = dev(yh=x, c=yl, x=yh, yl=c)
    swap_to = dev(yh=x, c=yl, x=yh, yl=1 - c)
    swap_from = dev(yh=x, c=1 - yl, x=yh, yl=c)
    lone = jnp.logical_and(yh == x, c == yl)

    barrier = pltpu.get_barrier_semaphore()
    peers = [right, left, pair_y, pair_c]
    peers += [dev(x=n, yl=m) for n in (xr, xl, xo) for m in (yl, 1 - yl)]
    peers += [dev(yh=yhs[r]) for r in (1, 2, 3)]
    peers += [swap_from]
    for peer in peers:
        pl.semaphore_signal(barrier, inc=1, device_id=peer, device_id_type=MESH)

    @pl.when(jnp.logical_not(lone))
    def _():
        pl.semaphore_signal(barrier, inc=1, device_id=swap, device_id_type=MESH)

    keys = {}
    sent = []

    def copy(key, src, dst, target):
        i = keys.setdefault(key, len(keys))
        return pltpu.make_async_remote_copy(
            src_ref=src, dst_ref=dst, send_sem=ssem.at[i], recv_sem=rsem.at[i],
            device_id=target, device_id_type=MESH,
        )

    def send(key, src, dst, target):
        cp = copy(key, src, dst, target)
        cp.start()
        sent.append(cp)

    def got(key, ref):
        copy(key, ref, ref, pair_c).wait_recv()

    load_in = pltpu.make_async_copy(in_ref, iv, lsem.at[0])
    load_bi = pltpu.make_async_copy(bi_ref, biv, lsem.at[1])
    load_b = pltpu.make_async_copy(b_ref, bv, lsem.at[3])
    for load in (load_b, load_bi, load_in):
        load.start()

    gs[...] = jnp.zeros_like(gs)
    for q in range(NX):
        for h in range(2):
            start = q * QUARTER + h * PAIR
            gs[q, h, 0:UNITS, :] = g_ref[:, start : start + PAIR]

    pl.semaphore_wait(barrier, jnp.where(lone, len(peers), len(peers) + 1))

    for n, xt in ((2, xo), (0, xr), (1, xl)):
        send(("a", n, 0), gs.at[xt], ga.at[x], dev(x=xt))
    for n, xt in ((2, xo), (0, xr), (1, xl)):
        send(("a", n, 1), gs.at[xt, 1], go.at[x], dev(x=xt, yl=1 - yl))
    send(("a", 3, 1), gs.at[x, 1], go.at[x], pair_y)
    ga[x] = gs[x]

    load_b.wait()
    row = lax.broadcasted_iota(jnp.int32, (COLS, 8 * GROUP), 0)
    lane = lax.broadcasted_iota(jnp.int32, (COLS, 8 * GROUP), 1)
    place = row + 60 * ((row * 3277) >> 16)
    for q in range(NX):
        picks[q] = jnp.where(lane == place + UNITS * q, 1.0, 0.0).astype(BF16)
    for part in range(3):
        total = None
        for q in range(NX):
            start = q * (BLOCK // NX) + part * COLS
            term = dot(bv[:, start : start + COLS], picks[q])
            total = term if total is None else total + term
        bb[x, :, part * 640 : (part + 1) * 640] = total.astype(BF16)
    for h in range(2):
        for way, half, xt in (("r", h, xr), ("l", 1 - h, xl)):
            ref = bb.at[x, pl.ds(half * HALF, HALF)]
            send(("b", way, half), ref, ref, dev(x=xt))

    class Item:
        def __init__(self, name, ref, both, far):
            self.name, self.ref, self.both, self.far = name, ref, both, far

        def at(self, mine, shift):
            col = yl if mine else 1 - yl
            return self.ref(col * NZ + lax.rem(z + shift + 2 * NZ, NZ))

        def hop(self, way, mine, k, shift):
            ref = self.at(mine, shift)
            send((self.name, way, mine, k), ref, ref, right if way == "r" else left)

        def across(self, shift):
            ref = self.at(True, shift)
            send((self.name, "y", shift), ref, ref, pair_y)

        def last(self, way, mine):
            return 6 if (way == self.far) == mine else 5

        def begin(self, mine):
            if mine or self.both:
                self.hop("r", mine, 1, 0)
                self.hop("l", mine, 1, 0)

        def step(self, k):
            for mine in (True, False) if self.both else (True,):
                for way, sign in (("r", -1), ("l", 1)):
                    if k <= self.last(way, mine):
                        got((self.name, way, mine, k), self.at(mine, sign * k))
                        if k < self.last(way, mine):
                            self.hop(way, mine, k + 1, sign * k)
                        if not self.both:
                            self.across(sign * k)
            if not self.both and k >= 2:
                self.crossed(k - 2)

        def crossed(self, k):
            ways = [(w, g) for w, g in (("r", -1), ("l", 1)) if k <= self.last(w, True)]
            for shift in [g * k for w, g in ways] if k else [0]:
                got((self.name, "y", shift), self.at(False, shift))

        def end(self):
            self.crossed(5)
            self.crossed(6)

    grads = [
        Item("g0", lambda s: gb.at[0, s], False, "r"),
        Item("g1", lambda s: gb.at[1, s], False, "l"),
        Item("g2", lambda s: gb.at[2, s], True, "r"),
        Item("g3", lambda s: gb.at[3, s], True, "l"),
    ]
    rot = Item("r", lambda s: rb.at[s], True, "l")

    load_bi.wait()
    load_in.wait()

    def slab(i, total):
        at = pl.ds(pl.multiple_of(i * 1536, 1536), 1536)
        return total + dot(iv[:, at], biv[:, at], ((1,), (1,)))

    tile = lax.fori_loop(0, DEPTH // 1536, slab, jnp.zeros((TOK, FEATS), F32))
    token = lax.broadcasted_iota(jnp.int32, (TOK, FEATS), 0)
    live = jnp.where(token < SLOT, cnt_ref[0], cnt_ref[1])
    tile = jnp.where((token & (SLOT - 1)) < live, tile, 0.0)
    rt[...] = tile.T.astype(BF16)
    own_copy = pltpu.make_async_copy(rt, rb.at[slot], lsem.at[4])

    swap_copy = copy(("swap",), rt, rb.at[c * NZ + z], swap)

    send(("swap", 2), rt, rb.at[c * NZ + z], swap_to)

    @pl.when(lone)
    def _():
        own_copy.start()
        own_copy.wait()

    @pl.when(jnp.logical_not(lone))
    def _():
        swap_copy.start()

    for n, xt in enumerate((xl, xr, xo)):
        got(("a", n, 0), ga.at[xt])
    prow = lax.broadcasted_iota(jnp.int32, (GROUP, NX * 32), 0)
    plane = lax.broadcasted_iota(jnp.int32, (GROUP, NX * 32), 1)
    unit = plane & 31
    hit = jnp.logical_and(prow == (plane >> 5) * UNITS + unit, unit < UNITS)
    pick = jnp.where(hit, 1.0, 0.0).astype(BF16)
    for h in range(2):
        packed = dot(pick, ga[:, h].reshape(NX * 32, PAIR)).astype(BF16)
        for ch in (2 * h, 2 * h + 1):
            gb[ch, slot] = packed[:, (ch % 2) * TW : (ch % 2 + 1) * TW]
            grads[ch].begin(True)
            if not grads[ch].both:
                grads[ch].across(0)
    for n, xt in enumerate((xl, xr, xo, x)):
        got(("a", n, 1), go.at[xt])
    packed = dot(pick, go[...].reshape(NX * 32, PAIR)).astype(BF16)
    for ch in (2, 3):
        gb[ch, (1 - yl) * NZ + z] = packed[:, (ch % 2) * TW : (ch % 2 + 1) * TW]
        grads[ch].begin(False)

    def rot_begin():
        @pl.when(jnp.logical_not(lone))
        def _():
            got(("swap",), rb.at[slot])

        rot.begin(True)
        got(("swap", 2), rot.at(False, 0))
        rot.begin(False)

    top, low = pl.ds(0, HALF), pl.ds(HALF, HALF)
    for it in range(1, 7):
        for item in grads:
            item.step(it)
        if it == 3:
            rot_begin()
        if it >= 4:
            rot.step(it - 3)
        if it == 3:
            got(("b", "r", 0), bb.at[xl, top])
            send(("b", "rr"), bb.at[xl, top], bb.at[xl, top], dev(x=xr))
            got(("b", "l", 1), bb.at[xr, low])
            send(("b", "ll"), bb.at[xr, low], bb.at[xr, low], dev(x=xl))
        if it == 5:
            got(("b", "l", 0), bb.at[xr, top])
            got(("b", "r", 1), bb.at[xl, low])
    grads[0].end()
    grads[1].end()
    got(("b", "rr"), bb.at[xo, pl.ds(0, HALF)])
    got(("b", "ll"), bb.at[xo, pl.ds(HALF, HALF)])

    early = len(sent)

    blocks = (xo, xr, xl, x)

    def multiply(i):
        for ch in range(0, CHUNKS, 2):
            both = [gb[ch + e].reshape(BLOCK, TW) for e in range(2)]
            part = dot(bb[blocks[i]], jnp.concatenate(both, axis=1))
            for e in range(2):
                for h in range(2):
                    at = slice(e * SLOT, (e + 1) * SLOT)
                    cb[i, h, ch + e] = part[h * HALF : (h + 1) * HALF, at]
        send(("c", i), cb.at[i, 1 - c], cr.at[i], pair_c)

    def scatter(i):
        got(("c", i), cr.at[i])
        for e in range(NH):
            ss[i, e] = (cb[i, c, e] + cr[i, e]).astype(BF16)
        for r in (2, 1, 3):
            send(("s", i, r), ss.at[i, yhs[r]], sr.at[i, r - 1], dev(yh=yhs[r]))

    def spread(i):
        total = cb[i, c, yh] + cr[i, yh]
        for r in (1, 3, 2):
            got(("s", i, r), sr.at[i, r - 1])
            total = total + sr[i, r - 1].astype(F32)
        ab[i, c, yh] = total.astype(BF16)
        mine = ab.at[i, c, yh]
        for r in (2, 1, 3):
            send(("t", i, r), mine, mine, dev(yh=yhs[r]))
        send(("u", i, 0), mine, mine, pair_c)

    def collect(i):
        for r in (1, 3, 2):
            ref = ab.at[i, c, yhs[NH - r]]
            got(("t", i, r), ref)
            send(("u", i, r), ref, ref, pair_c)

    def products(i):
        for r in range(NH):
            got(("u", i, r), ab.at[i, 1 - c, yhs[(NH - r) % NH]])
        for h in range(2):
            for f in range(3):
                total = None
                for e in range(NH):
                    first = (e // 2) * NZ + f * 4
                    at = slice((e % 2) * SLOT, (e % 2 + 1) * SLOT)
                    rows = rb[first : first + 4, :, at].reshape(4 * FEATS, SLOT)
                    term = dot(ab[i, h, e], rows, ((1,), (1,)))
                    total = term * term if total is None else total + term * term
                acc[i, pl.ds(h * HALF, HALF), pl.ds(f * 256, 256)] = total

    multiply(0)
    multiply(1)
    scatter(0)
    multiply(2)
    scatter(1)
    multiply(3)
    scatter(2)
    scatter(3)
    rot.step(4)
    spread(0)
    spread(1)
    rot.step(5)
    spread(2)
    collect(0)
    rot.step(6)
    spread(3)
    products(0)
    o1s[0] = acc[0, top].astype(BF16)
    send(("o1", "r"), o1s.at[0], o1r.at[0], dev(x=xr))
    o1s[1] = acc[0, low].astype(BF16)
    send(("o1", "l"), o1s.at[1], o1r.at[1], dev(x=xl))
    collect(1)
    products(1)
    o2s[0, 1] = acc[1, low].astype(BF16)
    send(("o2", "r", 1), o2s.at[0, 1], o2r.at[0, 1], dev(x=xr))
    collect(2)
    products(2)
    o2s[1, 0] = acc[2, top].astype(BF16)
    send(("o2", "l", 0), o2s.at[1, 0], o2r.at[1, 0], dev(x=xl))
    for cp in sent[:early]:
        cp.wait_send()
    got(("o1", "r"), o1r.at[0])
    o2s[0, 0] = (acc[1, top] + o1r[0].astype(F32)).astype(BF16)
    send(("o2", "r", 0), o2s.at[0, 0], o2r.at[0, 0], dev(x=xr))
    got(("o1", "l"), o1r.at[1])
    o2s[1, 1] = (acc[2, low] + o1r[1].astype(F32)).astype(BF16)
    send(("o2", "l", 1), o2s.at[1, 1], o2r.at[1, 1], dev(x=xl))
    collect(3)
    for cp in sent[early : len(sent) - 8]:
        cp.wait_send()
    late = len(sent) - 8
    products(3)
    for w, way in ((0, "r"), (1, "l")):
        for h in (1 - w, w):
            got(("o2", way, h), o2r.at[w, h])
    for h in range(2):
        rows = pl.ds(h * HALF, HALF)
        total = acc[3, rows] + o2r[0, h].astype(F32) + o2r[1, h].astype(F32)
        out_ref[rows, :] = total * FACTOR

    for cp in sent[late:]:
        cp.wait_send()

    @pl.when(jnp.logical_not(lone))
    def _():
        swap_copy.wait_send()

    assert len(keys) <= NSEM


def shards(out_grads, inputs, basis_grads, basis_inputs, counts):
    vmem = pl.BlockSpec(memory_space=pltpu.VMEM)
    hbm = pl.BlockSpec(memory_space=pl.ANY)
    return pl.pallas_call(
        kernel,
        out_shape=jax.ShapeDtypeStruct((COLS, WIDE), F32),
        in_specs=[vmem, hbm, hbm, hbm, pl.BlockSpec(memory_space=pltpu.SMEM)],
        out_specs=vmem,
        scratch_shapes=[
            pltpu.VMEM((NX, 2, 32, PAIR), BF16),
            pltpu.VMEM((NX, 2, 32, PAIR), BF16),
            pltpu.VMEM((NX, 32, PAIR), BF16),
            pltpu.VMEM((CHUNKS, SLOTS, GROUP, TW), BF16),
            pltpu.VMEM((NX, COLS, BLOCK), BF16),
            pltpu.VMEM((COLS, BLOCK), BF16),
            pltpu.VMEM((NX, COLS, 8 * GROUP), BF16),
            pltpu.VMEM((TOK, DEPTH), BF16),
            pltpu.VMEM((FEATS, DEPTH), BF16),
            pltpu.VMEM((FEATS, TOK), BF16),
            pltpu.VMEM((SLOTS, FEATS, TOK), BF16),
            pltpu.VMEM((NX, NC, NH, HALF, SLOT), F32),
            pltpu.VMEM((NX, NH, HALF, SLOT), F32),
            pltpu.VMEM((NX, NH, HALF, SLOT), BF16),
            pltpu.VMEM((NX, 3, HALF, SLOT), BF16),
            pltpu.VMEM((NX, NC, NH, HALF, SLOT), BF16),
            pltpu.VMEM((NX, COLS, WIDE), F32),
            pltpu.VMEM((2, HALF, WIDE), BF16),
            pltpu.VMEM((2, HALF, WIDE), BF16),
            pltpu.VMEM((2, 2, HALF, WIDE), BF16),
            pltpu.VMEM((2, 2, HALF, WIDE), BF16),
            pltpu.SemaphoreType.DMA((NSEM,)),
            pltpu.SemaphoreType.DMA((NSEM,)),
            pltpu.SemaphoreType.DMA((5,)),
        ],
        compiler_params=pltpu.CompilerParams(
            collective_id=0, has_side_effects=True, vmem_limit_bytes=53 * 1024 * 1024
        ),
        cost_estimate=pl.CostEstimate(
            flops=2_200_000_000, bytes_accessed=10_000_000, transcendentals=0
        ),
    )(out_grads, basis_grads.T, inputs, basis_inputs.T, counts)


def solution(mesh):
    placed = (P(("dp", "basis"), None), P("dp", None), P("dp", "basis"), P(None, "basis"), P("dp"))
    return jax.shard_map(
        shards, mesh=mesh, in_specs=placed, out_specs=P("basis", "dp"), check_vma=False
    )
```
